32 devices in a mesh: ax: 8 (over y, x, core), vt: 4 (over z).
Axes of the slice: x: 2, y: 2, z: 4, core: 2. Of those that a mesh axis runs over, the one named last changes fastest.
Arguments:
- fractions: float32 [2, 4, 4096, 128], P(None, 'vt', 'ax'), may hold values from 0 to 0.8
- motion_fields: float32 [4, 4, 4096, 128], P(None, 'vt', 'ax'), may hold values from -4 to 4
- new_home: int32 [4, 4096], P('vt', 'ax'), may hold values from 0 to 16383, as said below
- counts: int32 [4, 4096], P('vt', 'ax'), may hold values from 64 to 128, as said below
- neighbours: int32 [6, 4, 4096], P(None, 'vt', 'ax'), may hold values from -1 to 16383, as said below
- phase_ids: int32 [4, 4096, 128], P('vt', 'ax'), may hold values from 0 to 3
- growth_rates: float32 [4], replicated, may hold values from 0.5 to 5
Outputs:
- fractions_out: float32 [2, 4, 4096, 128], P(None, 'vt', 'ax')
- motion_out: float32 [4, 4, 4096, 128], P(None, 'vt', 'ax')
The draws below stay inside these ranges and needn't reach their ends.
Inputs may be any that keep to these rules, and one draw needn't show every extreme that they name: new_home is a permutation. A block keeps its slot, or moves to the slot with the same vertical index on the device whose ax index is one higher or one lower; a block that leaves a device is replaced in its slot by a block coming from the device it went to. At most 16 blocks pass from one device to one axial neighbour, and in every draw some pair of axially adjacent devices trades exactly 16 blocks each way. `neighbours`: -1 marks a pipe wall. The block across a face lies on a device whose ax index and whose vt index each differ by at most one from those of the block's own device; the relation is symmetric under opposite faces. A device's slots are numbered layer by layer along the pipe, 64 to a layer. Outside a device's lowest layer of slots at most 16 of its blocks have a block across some face on the device whose ax index is one lower, and outside its highest layer at most 16 have one on the device whose ax index is one higher; in every draw some device reaches 16 in each of these. The live cells of a block are its first counts cells; slot 0 of every device holds a full block.
All inputs are finite; a program needn't handle non-finite values.
Results may differ from the reference program's by a relative error of at most 0.0003.
Values sent between devices are 32-bit elements; how exact they have to be, the bound alone decides.
A program may use at most 128 MiB of HBM per device.

```python
import math
import jax
import jax.numpy as jnp

BLK_AX = 8
BLK_SPAN = 64
MOVES = 16
CELLS = 128
PHASES = 4
SLOTS = 4096
N_AX = 8
N_VT = 4


def locate(layer_at, axial_at, span_at):
    slots_dev = BLK_AX * BLK_SPAN
    return layer_at * SLOTS + axial_at // BLK_AX * slots_dev + axial_at % BLK_AX * BLK_SPAN + span_at


def layout(key):
    slots_dev = BLK_AX * BLK_SPAN
    total_blocks = N_VT * SLOTS
    pair_count = N_AX - 1
    base_key = jax.random.fold_in(key, 7)
    key_count, key_front, key_up, key_down = jax.random.split(base_key, 4)
    moving = jax.random.randint(key_count, (pair_count, N_VT), MOVES // 4, MOVES + 1)
    front_pair = jax.random.randint(key_front, (), 0, pair_count)
    moving = jnp.where((jnp.arange(pair_count) == front_pair)[:, None], MOVES, moving)
    span_index = jnp.arange(BLK_SPAN, dtype=jnp.int32)
    score_up = jax.random.randint(key_up, (pair_count, N_VT, BLK_SPAN), 0, 1 << 20) * BLK_SPAN + span_index
    score_down = jax.random.randint(key_down, (pair_count, N_VT, BLK_SPAN), 0, 1 << 20) * BLK_SPAN + span_index
    order_up = jnp.argsort(score_up, axis=-1).astype(jnp.int32)
    order_down = jnp.argsort(score_down, axis=-1).astype(jnp.int32)
    active = span_index[None, None, :] < moving[:, :, None]
    pair_index = jnp.arange(pair_count, dtype=jnp.int32)[:, None, None]
    layer_index = jnp.arange(N_VT, dtype=jnp.int32)[None, :, None]
    gid_up = layer_index * SLOTS + pair_index * slots_dev + (BLK_AX - 1) * BLK_SPAN + order_up
    gid_down = layer_index * SLOTS + (pair_index + 1) * slots_dev + order_down
    placed = jnp.arange(total_blocks, dtype=jnp.int32)
    placed = placed.at[jnp.where(active, gid_up, total_blocks).reshape(-1)].set(gid_down.reshape(-1), mode='drop')
    placed = placed.at[jnp.where(active, gid_down, total_blocks).reshape(-1)].set(gid_up.reshape(-1), mode='drop')
    block_id = jnp.arange(total_blocks, dtype=jnp.int32)
    layer_of = block_id // SLOTS
    along_pipe = block_id % SLOTS
    within = along_pipe % slots_dev
    axial_of = along_pipe // slots_dev * BLK_AX + within // BLK_SPAN
    span_of = within % BLK_SPAN
    offsets = ((0, -1, 0), (0, 1, 0), (-1, 0, 0), (1, 0, 0), (0, 0, -1), (0, 0, 1))
    linked_rows = []
    for layer_step, axial_step, span_step in offsets:
        layer_next = layer_of + layer_step
        axial_next = axial_of + axial_step
        span_next = span_of + span_step
        inside = (layer_next >= 0) & (layer_next < N_VT) & (axial_next >= 0) & (axial_next < N_AX * BLK_AX) & (span_next >= 0) & (span_next < BLK_SPAN)
        old_id = jnp.where(inside, locate(layer_next, axial_next, span_next), 0)
        linked_rows.append(jnp.where(inside, placed[old_id], -1))
    old_links = jnp.stack(linked_rows)
    inverse = jnp.zeros((total_blocks,), jnp.int32).at[placed].set(block_id)
    new_links = old_links[:, inverse]
    return (placed.reshape(N_VT, SLOTS), new_links.reshape(6, N_VT, SLOTS).astype(jnp.int32))


def draw_new_home(key, part):
    return layout(key)[0]


def draw_neighbours(key, part):
    return layout(key)[1]


def draw_counts(key, part):
    live_key = jax.random.fold_in(key, 11)
    drawn = jax.random.randint(live_key, (N_VT, SLOTS), 64, 129)
    first_slot = jnp.arange(SLOTS) % (BLK_AX * BLK_SPAN) == 0
    return jnp.where(first_slot[None, :], 128, drawn).astype(jnp.int32)


def place_ends(array, stream_key, least, high):
    dims = array.shape
    place = [jax.random.randint(jax.random.fold_in(stream_key, axis), (), 0, dims[axis]) for axis in range(len(dims))]
    array = array.at[tuple(place)].set(least)
    longest = dims.index(max(dims))
    place[longest] = (place[longest] + 1) % dims[longest]
    return array.at[tuple(place)].set(high)


def shard_levels(key, dims, shards, low, top_value):
    factor_of = 1.0
    for dim, shards_of in shards:
        heights = jax.random.uniform(jax.random.fold_in(jax.random.fold_in(key, 6), dim), (shards_of,), jnp.float32, low / len(shards), top_value / len(shards))
        factor_of = factor_of * jnp.repeat(jnp.exp(heights), dims[dim] // shards_of).reshape((-1,) + (1,) * (len(dims) - 1 - dim))
    return factor_of


def centred(key, shape, deviation, limit, shards=(), kind=jnp.bfloat16):
    level = shard_levels(key, shape, shards, -0.22, 0.18) if shards else 1.0
    values = jax.random.normal(key, shape, jnp.float32) * deviation * level
    return jnp.minimum(jnp.maximum(values, -limit), limit).astype(kind)


def setup_inputs(seed: int = 0) -> dict:
    streams_of = jax.random.split(jax.random.key(seed), 8)
    fractions = jnp.clip(0.8 * jax.random.uniform(streams_of[0], (2, N_VT, SLOTS, CELLS), jnp.float32) ** shard_levels(streams_of[0], (2, N_VT, SLOTS, CELLS), ((1, 4), (2, 8)), -0.2, 0.2), 0.0, 0.8)
    motion_fields = centred(streams_of[1], (4, N_VT, SLOTS, CELLS), 1.0, 4.0, ((1, 4), (2, 8)), jnp.float32)
    new_home = draw_new_home(jax.random.fold_in(streams_of[7], 71), 0)
    counts = draw_counts(jax.random.fold_in(streams_of[7], 71), 0)
    neighbours = draw_neighbours(jax.random.fold_in(streams_of[7], 71), 0)
    phase_ids = place_ends(jax.random.randint(streams_of[5], (N_VT, SLOTS, CELLS), 0, PHASES), jax.random.fold_in(streams_of[5], 1), 0, PHASES - 1).astype(jnp.int32)
    growth_rates = jnp.clip(jnp.exp(jax.random.uniform(streams_of[6], (PHASES,), jnp.float32, math.log(0.5), math.log(5.0))), 0.5, 5.0)
    return {"fractions": fractions, "motion_fields": motion_fields, "new_home": new_home, "counts": counts, "neighbours": neighbours, "phase_ids": phase_ids, "growth_rates": growth_rates}


axis_stride = (1, 32, 8)
axis_extent = (8, 4, 4)
time_step = 0.25


def face_flux(value, other, speed, other_speed, weight, outward_sign):
    outward = outward_sign * 0.5 * (speed + other_speed)
    return weight * (jnp.maximum(outward, 0.0) * value + jnp.minimum(outward, 0.0) * other)


def reference(fractions, motion_fields, new_home, counts, neighbours, phase_ids, growth_rates):
    block_total = new_home.size
    target = new_home.reshape(-1).astype(jnp.int32)
    frac_flat = fractions.reshape(2, block_total, 128)
    motion_flat = motion_fields.reshape(4, block_total, 128)
    frac_moved = jnp.zeros_like(frac_flat).at[:, target].set(frac_flat)
    motion_moved = jnp.zeros_like(motion_flat).at[:, target].set(motion_flat)
    position = jnp.arange(128, dtype=jnp.int32)
    live_cells = (position[None, :] < counts.reshape(-1)[:, None]).astype(jnp.float32)
    quantities = jnp.stack([frac_moved[0], frac_moved[1], motion_moved[0], motion_moved[1], motion_moved[2], live_cells])
    neighbour_at = neighbours.reshape(6, block_total).astype(jnp.int32)
    flux_liquid = jnp.zeros((block_total, 128), jnp.float32)
    flux_hydrate = jnp.zeros((block_total, 128), jnp.float32)
    for direction in range(6):
        along = direction // 2
        stride = axis_stride[along]
        extent = axis_extent[along]
        linked = neighbour_at[direction]
        present = linked >= 0
        other = jnp.where(present[None, :, None], quantities[:, jnp.maximum(linked, 0)], 0.0)
        coordinate = (position // stride) % extent
        if direction % 2 == 1:
            on_edge = coordinate == extent - 1
            from_other = jnp.roll(other, (extent - 1) * stride, axis=-1)
            inside = jnp.roll(quantities, -stride, axis=-1)
            outward_sign = 1.0
        else:
            on_edge = coordinate == 0
            from_other = jnp.roll(other, -(extent - 1) * stride, axis=-1)
            inside = jnp.roll(quantities, stride, axis=-1)
            outward_sign = -1.0
        near = jnp.where(on_edge[None, None, :], from_other, inside)
        weight = live_cells * near[5]
        speed = quantities[2 + along]
        flux_liquid = flux_liquid + face_flux(quantities[0], near[0], speed, near[2 + along], weight, outward_sign)
        flux_hydrate = flux_hydrate + face_flux(quantities[1], near[1], speed, near[2 + along], weight, outward_sign)
    phase_flat = phase_ids.reshape(block_total, 128)
    rate_cell = jnp.zeros((block_total, 128), jnp.float32)
    for phase_kind in range(growth_rates.shape[0]):
        rate_cell = rate_cell + jnp.where(phase_flat == phase_kind, growth_rates[phase_kind], 0.0)
    liquid = quantities[0]
    hydrate = quantities[1]
    growth = rate_cell * motion_moved[3] * liquid * (1.0 - hydrate)
    liquid_next = live_cells * (liquid - time_step * flux_liquid - time_step * growth)
    hydrate_next = live_cells * (hydrate - time_step * flux_hydrate + time_step * growth)
    fractions_out = jnp.stack([liquid_next, hydrate_next]).reshape(fractions.shape)
    motion_out = (motion_moved * live_cells[None]).reshape(motion_fields.shape)
    return fractions_out, motion_out
```

```python
import functools

import jax
import jax.numpy as jnp
from jax import lax
from jax.experimental import pallas as pl
from jax.experimental.pallas import tpu as pltpu
from jax.sharding import PartitionSpec as P

MOVES = 16
SPAN = 64
CELLS = 128
MESH = pl.DeviceIdType.MESH
HIGH = lax.Precision.HIGHEST
F32 = jnp.float32
BF16 = jnp.bfloat16

axis_stride = (1, 32, 8)
axis_extent = (8, 4, 4)
time_step = 0.25
table_of = (0, 0, 1, 2, 3, 4)
PACK = SPAN + MOVES
ROWS_AX = 5 * PACK + 8
ROWS_MV = 6 * MOVES + 8


def place_of(direction, member):
    return member + (4 if direction == 1 else 0)


def roll_lanes(x, shift):
    shift = shift % CELLS
    return x if shift == 0 else pltpu.roll(x, shift, 1)


def coordinates(rows):
    lane = lax.broadcasted_iota(jnp.int32, (rows, CELLS), 1)
    return (lane & 7, (lane >> 5) & 3, (lane >> 3) & 3)


def halves(x):
    hi = x.astype(BF16)
    return hi, (x - hi.astype(F32)).astype(BF16)


def kernel(na, nv, frac, mot, home, cnt, nb, phase, rates, fout, mout,
           cells, mv_send, mv_recv, mv_pay, tab, ax_send, ax_recv, vt_recv, win, acc, rowbuf, cols,
           mv_ss, mv_rs, ax_ss, ax_rs, vt_ss, vt_rs):
    slots = frac.shape[1]
    shift = slots.bit_length() - 1
    total = slots * na
    ax, vt = lax.axis_index("ax"), lax.axis_index("vt")

    def inside(a, v):
        return (a >= 0) & (a < na) & (v >= 0) & (v < nv)

    barrier = pltpu.get_barrier_semaphore()
    others = [(i, j) for i in (-1, 0, 1) for j in (-1, 0, 1) if (i, j) != (0, 0)]
    greeted = 0
    for i, j in others:
        there = inside(ax + i, vt + j)
        greeted = greeted + there.astype(jnp.int32)

        @pl.when(there)
        def _():
            pl.semaphore_signal(barrier, inc=1, device_id=(ax + i, vt + j), device_id_type=MESH)

    steps = (1, -1)

    def mover(s, peer):
        return pltpu.make_async_remote_copy(
            src_ref=mv_send.at[s], dst_ref=mv_recv.at[s], send_sem=mv_ss.at[s], recv_sem=mv_rs.at[s],
            device_id=peer, device_id_type=MESH)

    def axial(s, v, peer):
        return pltpu.make_async_remote_copy(
            src_ref=ax_send.at[s], dst_ref=ax_recv.at[s * 3 + v], send_sem=ax_ss.at[s * 3 + v],
            recv_sem=ax_rs.at[s * 3 + v], device_id=peer, device_id_type=MESH)

    def vertical(s, t, peer):
        return pltpu.make_async_remote_copy(
            src_ref=tab.at[t], dst_ref=vt_recv.at[s * 5 + t], send_sem=vt_ss.at[s * 5 + t],
            recv_sem=vt_rs.at[s * 5 + t], device_id=peer, device_id_type=MESH)

    slot_row = lax.broadcasted_iota(jnp.int32, (1, slots), 1)
    target = home[...]
    target_ax = (target >> shift) & (na - 1)
    linked = nb[...]
    linked_ax = jnp.where(linked >= 0, (linked >> shift) & (na - 1), -5)
    masks = [(target_ax == ax + 1), (target_ax == ax - 1)]
    reach_up = jnp.max((linked_ax == ax + 1).astype(jnp.int32), axis=0, keepdims=True) > 0
    reach_down = jnp.max((linked_ax == ax - 1).astype(jnp.int32), axis=0, keepdims=True) > 0
    masks += [reach_up & (slot_row < slots - SPAN), reach_down & (slot_row >= SPAN)]
    masks = [m.astype(F32) for m in masks]
    mask8 = jnp.concatenate(masks + [jnp.zeros((4, slots), F32)], axis=0)
    before = lax.broadcasted_iota(jnp.int32, (slots, slots), 0) < lax.broadcasted_iota(jnp.int32, (slots, slots), 1)
    rank = jnp.dot(mask8.astype(BF16), before.astype(F32).astype(BF16), preferred_element_type=F32)
    rank = jnp.where(mask8 > 0.0, rank, -1.0)

    rowbuf[...] = jnp.concatenate(
        [linked.astype(F32), cnt[...].astype(F32), jnp.zeros((1, slots), F32)], axis=0)
    cols[...] = rowbuf[...].T

    def one_hot(which, rows):
        m = (lax.broadcasted_iota(jnp.int32, (rows, slots), 0) & (MOVES - 1)).astype(F32)
        return (rank[which:which + 1] == m).astype(F32)

    def names(which, row):
        return lax.dot_general(
            jnp.broadcast_to(row, (8, slots)), one_hot(which, CELLS), (((1,), (1,)), ((), ())),
            precision=HIGH, preferred_element_type=F32)

    target_slot = (target & (slots - 1)).astype(F32) + 1.0
    global_row = (slot_row + (vt * total + ax * slots)).astype(F32) + 1.0
    pick = jnp.concatenate([one_hot(0, MOVES), one_hot(1, MOVES)], axis=0)
    for f in range(6):
        source = frac[f] if f < 2 else mot[f - 2]
        packed = jnp.dot(pick, source, precision=HIGH, preferred_element_type=F32)
        for s in range(2):
            mv_send[s, f * MOVES:(f + 1) * MOVES] = packed[s * MOVES:(s + 1) * MOVES]
    for s in range(2):
        mv_send[s, 6 * MOVES:] = names(s, target_slot)
        ax_send[s, 5 * PACK:] = names(2 + s, global_row)

    for s in range(2):
        @pl.when(jnp.logical_not(inside(ax - steps[s], vt)))
        def _():
            mv_recv[s] = jnp.zeros((ROWS_MV, CELLS), F32)

        @pl.when(jnp.logical_not(inside(ax, vt - steps[s])))
        def _():
            for t in range(5):
                vt_recv[s * 5 + t] = jnp.zeros((slots, CELLS), F32)

        for v in range(3):
            @pl.when(jnp.logical_not(inside(ax - steps[s], vt - (v - 1))))
            def _():
                ax_recv[s * 3 + v] = jnp.zeros((ROWS_AX, CELLS), F32)

    pl.semaphore_wait(barrier, greeted)
    for s in range(2):
        @pl.when(inside(ax + steps[s], vt))
        def _():
            mover(s, (ax + steps[s], vt)).start()

    mv_pay[...] = jnp.zeros_like(mv_pay)
    for s in range(2):
        @pl.when(inside(ax - steps[s], vt))
        def _():
            mover(s, (ax - steps[s], vt)).wait_recv()

    lane1 = lax.broadcasted_iota(jnp.int32, (1, CELLS), 1)
    arrivals = jnp.where(lane1 < MOVES, mv_recv[0, 6 * MOVES:6 * MOVES + 1],
                         jnp.where(lane1 < 2 * MOVES, mv_recv[1, 6 * MOVES:6 * MOVES + 1], 0.0)) - 1.0
    for f in range(6):
        for s in range(2):
            mv_pay[f, s * MOVES:(s + 1) * MOVES] = mv_recv[s, f * MOVES:(f + 1) * MOVES]

    chunk = 64

    @pl.loop(0, slots // chunk)
    def _(c):
        start = pl.multiple_of(c * chunk, chunk)
        rows = pl.ds(start, chunk)
        at = (lax.broadcasted_iota(jnp.int32, (chunk, CELLS), 0) + start).astype(F32)
        select = (at == arrivals).astype(F32)
        hit = jnp.max(select, axis=1, keepdims=True) > 0.0
        lane = lax.broadcasted_iota(jnp.int32, (chunk, CELLS), 1)
        live = (lane.astype(F32) < cols[rows, 6:7]).astype(F32)
        now = []
        for f in range(6):
            old = frac[f, rows] if f < 2 else mot[f - 2, rows]
            came = jnp.dot(select, mv_pay[f], precision=HIGH, preferred_element_type=F32)
            value = jnp.where(hit, came, old)
            cells[f, rows] = value
            now.append(value)
            if f >= 2:
                mout[f - 2, rows] = value * live
        coordinate = coordinates(chunk)
        for t in range(5):
            made = jnp.zeros((chunk, CELLS), F32)
            for d in range(6):
                if table_of[d] != t:
                    continue
                k = d // 2
                edge = axis_extent[k] - 1 if d % 2 == 0 else 0
                for member, value in enumerate((now[0], now[1], now[2 + k], live)):
                    p = place_of(d, member)
                    made = jnp.where(coordinate[k] == p, roll_lanes(value, (p - edge) * axis_stride[k]), made)
            tab[t, rows] = made
            hi, lo = halves(made)
            win[t, rows, :CELLS] = hi
            win[t, rows, CELLS:] = lo

    for t in range(5):
        for s in range(2):
            @pl.when(inside(ax, vt + steps[s]))
            def _():
                vertical(s, t, (ax, vt + steps[s])).start()

    pick = jnp.concatenate([one_hot(2, MOVES), one_hot(3, MOVES)], axis=0).astype(BF16)
    for t in range(5):
        both = jnp.dot(pick, win[t, :slots], preferred_element_type=F32)
        packed = both[:, :CELLS] + both[:, CELLS:]
        for s in range(2):
            first = slots - SPAN if s == 0 else 0
            ax_send[s, t * PACK:t * PACK + SPAN] = tab[t, first:first + SPAN]
            ax_send[s, t * PACK + SPAN:(t + 1) * PACK] = packed[s * MOVES:(s + 1) * MOVES]
    for s in range(2):
        for v in range(3):
            @pl.when(inside(ax + steps[s], vt + v - 1))
            def _():
                axial(s, v, (ax + steps[s], vt + v - 1)).start()

    tall = 128

    def gather(t, keys, fresh):
        @pl.loop(0, slots // tall)
        def _(c):
            rows = pl.ds(pl.multiple_of(c * tall, tall), tall)
            for d in range(6):
                if table_of[d] != t:
                    continue
                match = (cols[rows, d:d + 1] == keys).astype(F32).astype(BF16)
                both = jnp.dot(match, win[t, :slots], preferred_element_type=F32)
                both = both[:, :CELLS] + both[:, CELLS:]
                if fresh:
                    acc[d, rows] = both
                else:
                    acc[d, rows] += both

    for t in range(5):
        gather(t, global_row - 1.0, True)

    for s in range(2):
        for v in range(3):
            @pl.when(inside(ax - steps[s], vt - (v - 1)))
            def _():
                axial(s, v, (ax - steps[s], vt - (v - 1))).wait_recv()
    layer_keys = jnp.full((1, slots), -2.0, F32)
    which = slot_row >> (SPAN.bit_length() - 1)
    within = slot_row & (SPAN - 1)
    for s in range(2):
        for v in range(3):
            w = s * 3 + v
            base = (vt - (v - 1)) * total + (ax - steps[s]) * slots + (slots - SPAN if s == 0 else 0)
            layer_keys = jnp.where(which == w, (within + base).astype(F32), layer_keys)
    other_keys = jnp.full((1, CELLS), -2.0, F32)
    for w in range(6):
        row = ax_recv[w, 5 * PACK:5 * PACK + 1]
        row = jnp.where(row > 0.0, row - 1.0, -2.0)
        other_keys = jnp.where((lane1 >> 4) == w, row, other_keys)
    ax_keys = jnp.concatenate([layer_keys[:, :6 * SPAN], other_keys], axis=1)
    for t in range(5):
        for w in range(6):
            hi, lo = halves(ax_recv[w, t * PACK:t * PACK + SPAN])
            win[t, w * SPAN:(w + 1) * SPAN, :CELLS] = hi
            win[t, w * SPAN:(w + 1) * SPAN, CELLS:] = lo
            first = 6 * SPAN + w * MOVES
            hi, lo = halves(ax_recv[w, t * PACK + SPAN:(t + 1) * PACK])
            win[t, first:first + MOVES, :CELLS] = hi
            win[t, first:first + MOVES, CELLS:] = lo
        win[t, 6 * PACK:] = jnp.zeros((slots - 6 * PACK, 2 * CELLS), BF16)
        gather(t, ax_keys, False)

    for t in range(5):
        for s in range(2):
            @pl.when(inside(ax, vt - steps[s]))
            def _():
                vertical(s, t, (ax, vt - steps[s])).wait_recv()

            @pl.loop(0, slots // tall)
            def _(c):
                rows = pl.ds(pl.multiple_of(c * tall, tall), tall)
                hi, lo = halves(vt_recv[s * 5 + t, rows])
                win[t, rows, :CELLS] = hi
                win[t, rows, CELLS:] = lo

            gather(t, (slot_row + ((vt - steps[s]) * total + ax * slots)).astype(F32), False)

    small = 32

    @pl.loop(0, slots // small)
    def _(c):
        rows = pl.ds(pl.multiple_of(c * small, small), small)
        lane = lax.broadcasted_iota(jnp.int32, (small, CELLS), 1)
        live = (lane.astype(F32) < cols[rows, 6:7]).astype(F32)
        coordinate = coordinates(small)
        liquid, hydrate = cells[0, rows], cells[1, rows]
        flux_l = jnp.zeros((small, CELLS), F32)
        flux_h = jnp.zeros((small, CELLS), F32)
        for d in range(6):
            k = d // 2
            stride, extent = axis_stride[k], axis_extent[k]
            edge = 0 if d % 2 == 0 else extent - 1
            step = stride if d % 2 == 0 else -stride
            got = acc[d, rows]
            speed = cells[2 + k, rows]
            near = [
                jnp.where(coordinate[k] == edge, roll_lanes(got, (edge - place_of(d, m)) * stride), roll_lanes(value, step))
                for m, value in enumerate((liquid, hydrate, speed, live))
            ]
            outward = (1.0 if d % 2 else -1.0) * 0.5 * (speed + near[2])
            weight = live * near[3]
            out, into = weight * jnp.maximum(outward, 0.0), weight * jnp.minimum(outward, 0.0)
            flux_l = flux_l + (out * liquid + into * near[0])
            flux_h = flux_h + (out * hydrate + into * near[1])
        rate = jnp.zeros((small, CELLS), F32)
        kinds = phase[rows]
        for kind in range(rates.shape[0]):
            rate = jnp.where(kinds == kind, rates[kind], rate)
        growth = rate * cells[5, rows] * liquid * (1.0 - hydrate)
        fout[0, rows] = live * (liquid - time_step * flux_l - time_step * growth)
        fout[1, rows] = live * (hydrate - time_step * flux_h + time_step * growth)

    for s in range(2):
        @pl.when(inside(ax + steps[s], vt))
        def _():
            mover(s, (ax + steps[s], vt)).wait_send()

        for v in range(3):
            @pl.when(inside(ax + steps[s], vt + v - 1))
            def _():
                axial(s, v, (ax + steps[s], vt + v - 1)).wait_send()

        for t in range(5):
            @pl.when(inside(ax, vt + steps[s]))
            def _():
                vertical(s, t, (ax, vt + steps[s])).wait_send()


def on_device(fractions, motion_fields, new_home, counts, neighbours, phase_ids, growth_rates):
    na, nv = lax.axis_size("ax"), lax.axis_size("vt")
    slots = fractions.shape[2]
    vmem = pl.BlockSpec(memory_space=pltpu.VMEM)
    fout, mout = pl.pallas_call(
        functools.partial(kernel, na, nv),
        out_shape=(jax.ShapeDtypeStruct((2, slots, CELLS), F32), jax.ShapeDtypeStruct((4, slots, CELLS), F32)),
        in_specs=[vmem] * 6 + [pl.BlockSpec(memory_space=pltpu.SMEM)],
        out_specs=(vmem, vmem),
        scratch_shapes=[
            pltpu.VMEM((6, slots, CELLS), F32),
            pltpu.VMEM((2, ROWS_MV, CELLS), F32),
            pltpu.VMEM((2, ROWS_MV, CELLS), F32),
            pltpu.VMEM((6, CELLS, CELLS), F32),
            pltpu.VMEM((5, slots, CELLS), F32),
            pltpu.VMEM((2, ROWS_AX, CELLS), F32),
            pltpu.VMEM((6, ROWS_AX, CELLS), F32),
            pltpu.VMEM((10, slots, CELLS), F32),
            pltpu.VMEM((5, slots, 2 * CELLS), BF16),
            pltpu.VMEM((6, slots, CELLS), F32),
            pltpu.VMEM((8, slots), F32),
            pltpu.VMEM((slots, 8), F32),
            pltpu.SemaphoreType.DMA((2,)),
            pltpu.SemaphoreType.DMA((2,)),
            pltpu.SemaphoreType.DMA((6,)),
            pltpu.SemaphoreType.DMA((6,)),
            pltpu.SemaphoreType.DMA((10,)),
            pltpu.SemaphoreType.DMA((10,)),
        ],
        compiler_params=pltpu.CompilerParams(
            collective_id=0, has_side_effects=True, vmem_limit_bytes=40 * 1024 * 1024),
    )(fractions[:, 0], motion_fields[:, 0], new_home, counts, neighbours[:, 0], phase_ids[0], growth_rates)
    return fout[:, None], mout[:, None]


def solution(mesh):
    in_specs = (
        P(None, "vt", "ax", None),
        P(None, "vt", "ax", None),
        P("vt", "ax"),
        P("vt", "ax"),
        P(None, "vt", "ax"),
        P("vt", "ax", None),
        P(),
    )
    out_specs = (P(None, "vt", "ax", None), P(None, "vt", "ax", None))
    return jax.shard_map(
        on_device, mesh=mesh, in_specs=in_specs, out_specs=out_specs, check_vma=False
    )
```

```python
import functools

import jax
import jax.numpy as jnp
from jax import lax
from jax.experimental import pallas as pl
from jax.experimental.pallas import tpu as pltpu
from jax.sharding import PartitionSpec as P

MOVES = 16
SPAN = 64
CELLS = 128
MESH = pl.DeviceIdType.MESH
HIGH = lax.Precision.HIGHEST
F32 = jnp.float32
BF16 = jnp.bfloat16

axis_stride = (1, 32, 8)
axis_extent = (8, 4, 4)
time_step = 0.25
table_of = (0, 0, 1, 2, 3, 4)
PACK = SPAN + MOVES
ROWS_AX = 5 * PACK + 8
ROWS_MV = 6 * MOVES + 8


def place_of(direction, member):
    return member + (4 if direction == 1 else 0)


def roll_lanes(x, shift):
    shift = shift % CELLS
    return x if shift == 0 else pltpu.roll(x, shift, 1)


def coordinates(rows):
    lane = lax.broadcasted_iota(jnp.int32, (rows, CELLS), 1)
    return (lane & 7, (lane >> 5) & 3, (lane >> 3) & 3)


def halves(x):
    hi = x.astype(BF16)
    return hi, (x - hi.astype(F32)).astype(BF16)


PIECES = 4
COUNT_LANE = 45


def quarter_shift(yh, zh, edge):
    return 1 + yh + 2 * zh - edge + 8 * (1 - 2 * yh) + 32 * (1 - 2 * zh)


def pack_union(liquid, hydrate, speeds, count):
    x, z, y = coordinates(liquid.shape[0])
    core = (y >= 1) & (y <= 2) & (z >= 1) & (z <= 2)
    kept = []
    for value, edge in ((liquid, 0), (hydrate, 7)):
        for yh in range(2):
            for zh in range(2):
                value = jnp.where(core & (x == 1 + yh + 2 * zh), roll_lanes(speeds[0], quarter_shift(yh, zh, edge)), value)
        kept.append(value)
    lane = lax.broadcasted_iota(jnp.int32, liquid.shape, 1)
    kept[0] = jnp.where(lane == COUNT_LANE, count, kept[0])
    third = speeds[1]
    middle = (z >= 1) & (z <= 2)
    for zh in range(2):
        for far in range(2):
            third = jnp.where(middle & (y == 2 * zh + far),
                              roll_lanes(speeds[2], 32 * (1 - 2 * zh) + 8 * (2 * zh - 2 * far)), third)
    return kept[0], kept[1], third


def union_tables(first, second, third):
    rows = first.shape[0]
    coordinate = coordinates(rows)
    x, z, y = coordinate
    lane = lax.broadcasted_iota(jnp.int32, (rows, CELLS), 1)
    live = (lane.astype(F32) < first[:, COUNT_LANE:COUNT_LANE + 1]).astype(F32)
    tables = [jnp.zeros((rows, CELLS), F32) for _ in range(5)]
    for d in range(6):
        t, k = table_of[d], d // 2
        edge = axis_extent[k] - 1 if d % 2 == 0 else 0
        made = tables[t]
        for member, value in enumerate((first, second, None, live)):
            p = place_of(d, member)
            there = coordinate[k] == p
            if member != 2:
                made = jnp.where(there, roll_lanes(value, (p - edge) * axis_stride[k]), made)
            elif k == 0:
                held = second if edge else first
                for yh in range(2):
                    for zh in range(2):
                        made = jnp.where(there & ((y >> 1) == yh) & ((z >> 1) == zh),
                                         roll_lanes(held, p - edge - quarter_shift(yh, zh, edge)), made)
            elif k == 1:
                made = jnp.where(there, roll_lanes(third, (p - edge) * 32), made)
            else:
                far = 1 if edge else 0
                for zh in range(2):
                    made = jnp.where(there & ((z >> 1) == zh),
                                     roll_lanes(third, 8 * (p - 2 * zh - far) - 32 * (1 - 2 * zh)), made)
        tables[t] = made
    return tables


def kernel(na, nv, frac, mot, home, cnt, nb, phase, rates, fout, mout,
           cells, mv_send, mv_recv, mv_pay, tab, vt_send, ax_send, ax_recv, vt_recv, win, acc, rowbuf, cols,
           mv_ss, mv_rs, ax_ss, ax_rs, vt_ss, vt_rs):
    slots = frac.shape[1]
    shift = slots.bit_length() - 1
    total = slots * na
    ax, vt = lax.axis_index("ax"), lax.axis_index("vt")

    def inside(a, v):
        return (a >= 0) & (a < na) & (v >= 0) & (v < nv)

    barrier = pltpu.get_barrier_semaphore()
    others = [(i, j) for i in (-1, 0, 1) for j in (-1, 0, 1) if (i, j) != (0, 0)]
    greeted = 0
    for i, j in others:
        there = inside(ax + i, vt + j)
        greeted = greeted + there.astype(jnp.int32)

        @pl.when(there)
        def _():
            pl.semaphore_signal(barrier, inc=1, device_id=(ax + i, vt + j), device_id_type=MESH)

    steps = (1, -1)

    def mover(s, peer):
        return pltpu.make_async_remote_copy(
            src_ref=mv_send.at[s], dst_ref=mv_recv.at[s], send_sem=mv_ss.at[s], recv_sem=mv_rs.at[s],
            device_id=peer, device_id_type=MESH)

    def axial(s, v, peer):
        return pltpu.make_async_remote_copy(
            src_ref=ax_send.at[s], dst_ref=ax_recv.at[s * 3 + v], send_sem=ax_ss.at[s * 3 + v],
            recv_sem=ax_rs.at[s * 3 + v], device_id=peer, device_id_type=MESH)

    piece = slots // PIECES

    def vertical(s, q, peer):
        return pltpu.make_async_remote_copy(
            src_ref=vt_send.at[q], dst_ref=vt_recv.at[s * PIECES + q], send_sem=vt_ss.at[s * PIECES + q],
            recv_sem=vt_rs.at[s * PIECES + q], device_id=peer, device_id_type=MESH)

    slot_row = lax.broadcasted_iota(jnp.int32, (1, slots), 1)
    target = home[...]
    target_ax = (target >> shift) & (na - 1)
    linked = nb[...]
    linked_ax = jnp.where(linked >= 0, (linked >> shift) & (na - 1), -5)
    masks = [(target_ax == ax + 1), (target_ax == ax - 1)]
    reach_up = jnp.max((linked_ax == ax + 1).astype(jnp.int32), axis=0, keepdims=True) > 0
    reach_down = jnp.max((linked_ax == ax - 1).astype(jnp.int32), axis=0, keepdims=True) > 0
    masks += [reach_up & (slot_row < slots - SPAN), reach_down & (slot_row >= SPAN)]
    masks = [m.astype(F32) for m in masks]
    mask8 = jnp.concatenate(masks + [jnp.zeros((4, slots), F32)], axis=0)
    before = lax.broadcasted_iota(jnp.int32, (slots, slots), 0) < lax.broadcasted_iota(jnp.int32, (slots, slots), 1)
    rank = jnp.dot(mask8.astype(BF16), before.astype(F32).astype(BF16), preferred_element_type=F32)
    rank = jnp.where(mask8 > 0.0, rank, -1.0)

    rowbuf[...] = jnp.concatenate(
        [linked.astype(F32), cnt[...].astype(F32), jnp.zeros((1, slots), F32)], axis=0)
    cols[...] = rowbuf[...].T

    def one_hot(which, rows):
        m = (lax.broadcasted_iota(jnp.int32, (rows, slots), 0) & (MOVES - 1)).astype(F32)
        return (rank[which:which + 1] == m).astype(F32)

    def names(which, row):
        return lax.dot_general(
            jnp.broadcast_to(row, (8, slots)), one_hot(which, CELLS), (((1,), (1,)), ((), ())),
            precision=HIGH, preferred_element_type=F32)

    target_slot = (target & (slots - 1)).astype(F32) + 1.0
    global_row = (slot_row + (vt * total + ax * slots)).astype(F32) + 1.0
    pick = jnp.concatenate([one_hot(0, MOVES), one_hot(1, MOVES)], axis=0)
    for f in range(6):
        source = frac[f] if f < 2 else mot[f - 2]
        packed = jnp.dot(pick, source, precision=HIGH, preferred_element_type=F32)
        for s in range(2):
            mv_send[s, f * MOVES:(f + 1) * MOVES] = packed[s * MOVES:(s + 1) * MOVES]
    for s in range(2):
        mv_send[s, 6 * MOVES:] = names(s, target_slot)
        ax_send[s, 5 * PACK:] = names(2 + s, global_row)

    for s in range(2):
        @pl.when(jnp.logical_not(inside(ax - steps[s], vt)))
        def _():
            mv_recv[s] = jnp.zeros((ROWS_MV, CELLS), F32)

        @pl.when(jnp.logical_not(inside(ax, vt - steps[s])))
        def _():
            for q in range(PIECES):
                vt_recv[s * PIECES + q] = jnp.zeros((3, piece, CELLS), F32)

        for v in range(3):
            @pl.when(jnp.logical_not(inside(ax - steps[s], vt - (v - 1))))
            def _():
                ax_recv[s * 3 + v] = jnp.zeros((ROWS_AX, CELLS), F32)

    pl.semaphore_wait(barrier, greeted)
    for s in range(2):
        @pl.when(inside(ax + steps[s], vt))
        def _():
            mover(s, (ax + steps[s], vt)).start()

    mv_pay[...] = jnp.zeros_like(mv_pay)
    for s in range(2):
        @pl.when(inside(ax - steps[s], vt))
        def _():
            mover(s, (ax - steps[s], vt)).wait_recv()

    lane1 = lax.broadcasted_iota(jnp.int32, (1, CELLS), 1)
    arrivals = jnp.where(lane1 < MOVES, mv_recv[0, 6 * MOVES:6 * MOVES + 1],
                         jnp.where(lane1 < 2 * MOVES, mv_recv[1, 6 * MOVES:6 * MOVES + 1], 0.0)) - 1.0
    for f in range(6):
        for s in range(2):
            mv_pay[f, s * MOVES:(s + 1) * MOVES] = mv_recv[s, f * MOVES:(f + 1) * MOVES]

    chunk = 64

    def settle(q, c):
        start = pl.multiple_of(q * piece + c * chunk, chunk)
        part = pl.ds(pl.multiple_of(c * chunk, chunk), chunk)
        rows = pl.ds(start, chunk)
        at = (lax.broadcasted_iota(jnp.int32, (chunk, CELLS), 0) + start).astype(F32)
        select = (at == arrivals).astype(F32)
        hit = jnp.max(select, axis=1, keepdims=True) > 0.0
        lane = lax.broadcasted_iota(jnp.int32, (chunk, CELLS), 1)
        live = (lane.astype(F32) < cols[rows, 6:7]).astype(F32)
        now = []
        for f in range(6):
            old = frac[f, rows] if f < 2 else mot[f - 2, rows]
            came = jnp.dot(select, mv_pay[f], precision=HIGH, preferred_element_type=F32)
            value = jnp.where(hit, came, old)
            cells[f, rows] = value
            now.append(value)
            if f >= 2:
                mout[f - 2, rows] = value * live
        coordinate = coordinates(chunk)
        for t in range(5):
            made = jnp.zeros((chunk, CELLS), F32)
            for d in range(6):
                if table_of[d] != t:
                    continue
                k = d // 2
                edge = axis_extent[k] - 1 if d % 2 == 0 else 0
                for member, value in enumerate((now[0], now[1], now[2 + k], live)):
                    p = place_of(d, member)
                    made = jnp.where(coordinate[k] == p, roll_lanes(value, (p - edge) * axis_stride[k]), made)
            tab[t, rows] = made
            hi, lo = halves(made)
            win[t, rows, :CELLS] = hi
            win[t, rows, CELLS:] = lo
        union = pack_union(now[0], now[1], now[2:5], cols[rows, 6:7])
        for r in range(3):
            vt_send[q, r, part] = union[r]

    for q in range(PIECES):
        pl.loop(0, piece // chunk)(functools.partial(settle, q))
        for s in range(2):
            @pl.when(inside(ax, vt + steps[s]))
            def _():
                vertical(s, q, (ax, vt + steps[s])).start()

    pick = jnp.concatenate([one_hot(2, MOVES), one_hot(3, MOVES)], axis=0).astype(BF16)
    for t in range(5):
        both = jnp.dot(pick, win[t, :slots], preferred_element_type=F32)
        packed = both[:, :CELLS] + both[:, CELLS:]
        for s in range(2):
            first = slots - SPAN if s == 0 else 0
            ax_send[s, t * PACK:t * PACK + SPAN] = tab[t, first:first + SPAN]
            ax_send[s, t * PACK + SPAN:(t + 1) * PACK] = packed[s * MOVES:(s + 1) * MOVES]
    for s in range(2):
        for v in range(3):
            @pl.when(inside(ax + steps[s], vt + v - 1))
            def _():
                axial(s, v, (ax + steps[s], vt + v - 1)).start()

    def gather(t, keys, fresh):
        depth = keys.shape[1]
        for d in range(6):
            if table_of[d] != t:
                continue
            match = (cols[:, d:d + 1] == keys).astype(F32).astype(BF16)
            both = jnp.dot(match, win[t, :depth], preferred_element_type=F32)
            both = both[:, :CELLS] + both[:, CELLS:]
            if fresh:
                acc[d] = both
            else:
                acc[d] += both

    for t in range(5):
        gather(t, global_row - 1.0, True)

    for s in range(2):
        for v in range(3):
            @pl.when(inside(ax - steps[s], vt - (v - 1)))
            def _():
                axial(s, v, (ax - steps[s], vt - (v - 1))).wait_recv()
    layer_keys = jnp.full((1, slots), -2.0, F32)
    which = slot_row >> (SPAN.bit_length() - 1)
    within = slot_row & (SPAN - 1)
    for s in range(2):
        for v in range(3):
            w = s * 3 + v
            base = (vt - (v - 1)) * total + (ax - steps[s]) * slots + (slots - SPAN if s == 0 else 0)
            layer_keys = jnp.where(which == w, (within + base).astype(F32), layer_keys)
    other_keys = jnp.full((1, CELLS), -2.0, F32)
    for w in range(6):
        row = ax_recv[w, 5 * PACK:5 * PACK + 1]
        row = jnp.where(row > 0.0, row - 1.0, -2.0)
        other_keys = jnp.where((lane1 >> 4) == w, row, other_keys)
    ax_keys = jnp.concatenate([layer_keys[:, :6 * SPAN], other_keys], axis=1)
    for t in range(5):
        for w in range(6):
            hi, lo = halves(ax_recv[w, t * PACK:t * PACK + SPAN])
            win[t, w * SPAN:(w + 1) * SPAN, :CELLS] = hi
            win[t, w * SPAN:(w + 1) * SPAN, CELLS:] = lo
            first = 6 * SPAN + w * MOVES
            hi, lo = halves(ax_recv[w, t * PACK + SPAN:(t + 1) * PACK])
            win[t, first:first + MOVES, :CELLS] = hi
            win[t, first:first + MOVES, CELLS:] = lo
        win[t, 6 * PACK:] = jnp.zeros((slots - 6 * PACK, 2 * CELLS), BF16)
        gather(t, ax_keys, False)

    piece_row = lax.broadcasted_iota(jnp.int32, (1, piece), 1)
    unpack = 32
    for q in range(PIECES):
        keys = []
        for s in range(2):
            @pl.when(inside(ax, vt - steps[s]))
            def _():
                vertical(s, q, (ax, vt - steps[s])).wait_recv()

            @pl.loop(0, piece // unpack)
            def _(c):
                rows = pl.ds(pl.multiple_of(c * unpack, unpack), unpack)
                to = pl.ds(pl.multiple_of(s * piece + c * unpack, unpack), unpack)
                tables = union_tables(*[vt_recv[s * PIECES + q, r, rows] for r in range(3)])
                for t in range(5):
                    hi, lo = halves(tables[t])
                    win[t, to, :CELLS] = hi
                    win[t, to, CELLS:] = lo

            keys.append((piece_row + ((vt - steps[s]) * total + ax * slots + q * piece)).astype(F32))
        keys = jnp.concatenate(keys, axis=1)
        for t in range(5):
            gather(t, keys, False)

    small = 32

    @pl.loop(0, slots // small)
    def _(c):
        rows = pl.ds(pl.multiple_of(c * small, small), small)
        lane = lax.broadcasted_iota(jnp.int32, (small, CELLS), 1)
        live = (lane.astype(F32) < cols[rows, 6:7]).astype(F32)
        coordinate = coordinates(small)
        liquid, hydrate = cells[0, rows], cells[1, rows]
        flux_l = jnp.zeros((small, CELLS), F32)
        flux_h = jnp.zeros((small, CELLS), F32)
        for d in range(6):
            k = d // 2
            stride, extent = axis_stride[k], axis_extent[k]
            edge = 0 if d % 2 == 0 else extent - 1
            step = stride if d % 2 == 0 else -stride
            got = acc[d, rows]
            speed = cells[2 + k, rows]
            near = [
                jnp.where(coordinate[k] == edge, roll_lanes(got, (edge - place_of(d, m)) * stride), roll_lanes(value, step))
                for m, value in enumerate((liquid, hydrate, speed, live))
            ]
            outward = (1.0 if d % 2 else -1.0) * 0.5 * (speed + near[2])
            weight = live * near[3]
            out, into = weight * jnp.maximum(outward, 0.0), weight * jnp.minimum(outward, 0.0)
            flux_l = flux_l + (out * liquid + into * near[0])
            flux_h = flux_h + (out * hydrate + into * near[1])
        rate = jnp.zeros((small, CELLS), F32)
        kinds = phase[rows]
        for kind in range(rates.shape[0]):
            rate = jnp.where(kinds == kind, rates[kind], rate)
        growth = rate * cells[5, rows] * liquid * (1.0 - hydrate)
        fout[0, rows] = live * (liquid - time_step * flux_l - time_step * growth)
        fout[1, rows] = live * (hydrate - time_step * flux_h + time_step * growth)

    for s in range(2):
        @pl.when(inside(ax + steps[s], vt))
        def _():
            mover(s, (ax + steps[s], vt)).wait_send()

        for v in range(3):
            @pl.when(inside(ax + steps[s], vt + v - 1))
            def _():
                axial(s, v, (ax + steps[s], vt + v - 1)).wait_send()

        for q in range(PIECES):
            @pl.when(inside(ax, vt + steps[s]))
            def _():
                vertical(s, q, (ax, vt + steps[s])).wait_send()


def on_device(fractions, motion_fields, new_home, counts, neighbours, phase_ids, growth_rates):
    na, nv = lax.axis_size("ax"), lax.axis_size("vt")
    slots = fractions.shape[2]
    vmem = pl.BlockSpec(memory_space=pltpu.VMEM)
    fout, mout = pl.pallas_call(
        functools.partial(kernel, na, nv),
        out_shape=(jax.ShapeDtypeStruct((2, slots, CELLS), F32), jax.ShapeDtypeStruct((4, slots, CELLS), F32)),
        in_specs=[vmem] * 6 + [pl.BlockSpec(memory_space=pltpu.SMEM)],
        out_specs=(vmem, vmem),
        scratch_shapes=[
            pltpu.VMEM((6, slots, CELLS), F32),
            pltpu.VMEM((2, ROWS_MV, CELLS), F32),
            pltpu.VMEM((2, ROWS_MV, CELLS), F32),
            pltpu.VMEM((6, CELLS, CELLS), F32),
            pltpu.VMEM((5, slots, CELLS), F32),
            pltpu.VMEM((PIECES, 3, slots // PIECES, CELLS), F32),
            pltpu.VMEM((2, ROWS_AX, CELLS), F32),
            pltpu.VMEM((6, ROWS_AX, CELLS), F32),
            pltpu.VMEM((2 * PIECES, 3, slots // PIECES, CELLS), F32),
            pltpu.VMEM((5, slots, 2 * CELLS), BF16),
            pltpu.VMEM((6, slots, CELLS), F32),
            pltpu.VMEM((8, slots), F32),
            pltpu.VMEM((slots, 8), F32),
            pltpu.SemaphoreType.DMA((2,)),
            pltpu.SemaphoreType.DMA((2,)),
            pltpu.SemaphoreType.DMA((6,)),
            pltpu.SemaphoreType.DMA((6,)),
            pltpu.SemaphoreType.DMA((2 * PIECES,)),
            pltpu.SemaphoreType.DMA((2 * PIECES,)),
        ],
        compiler_params=pltpu.CompilerParams(
            collective_id=0, has_side_effects=True, vmem_limit_bytes=40 * 1024 * 1024),
    )(fractions[:, 0], motion_fields[:, 0], new_home, counts, neighbours[:, 0], phase_ids[0], growth_rates)
    return fout[:, None], mout[:, None]


def solution(mesh):
    in_specs = (
        P(None, "vt", "ax", None),
        P(None, "vt", "ax", None),
        P("vt", "ax"),
        P("vt", "ax"),
        P(None, "vt", "ax"),
        P("vt", "ax", None),
        P(),
    )
    out_specs = (P(None, "vt", "ax", None), P(None, "vt", "ax", None))
    return jax.shard_map(
        on_device, mesh=mesh, in_specs=in_specs, out_specs=out_specs, check_vma=False
    )
```

```python
import functools

import jax
import jax.numpy as jnp
from jax import lax
from jax.experimental import pallas as pl
from jax.experimental.pallas import tpu as pltpu
from jax.sharding import PartitionSpec as P

MOVES = 16
SPAN = 64
CELLS = 128
MESH = pl.DeviceIdType.MESH
HIGH = lax.Precision.HIGHEST
F32 = jnp.float32
BF16 = jnp.bfloat16

axis_stride = (1, 32, 8)
axis_extent = (8, 4, 4)
time_step = 0.25
table_of = (0, 0, 1, 2, 3, 4)
PACK = SPAN + MOVES
ROWS_AX = 3 * PACK + 8
ROWS_MV = 6 * MOVES + 8


def place_of(direction, member):
    return member + (4 if direction == 1 else 0)


def roll_lanes(x, shift):
    shift = shift % CELLS
    return x if shift == 0 else pltpu.roll(x, shift, 1)


def coordinates(rows):
    lane = lax.broadcasted_iota(jnp.int32, (rows, CELLS), 1)
    return (lane & 7, (lane >> 5) & 3, (lane >> 3) & 3)


def halves(x):
    hi = x.astype(BF16)
    return hi, (x - hi.astype(F32)).astype(BF16)


PIECES = 4
COUNT_LANE = 45


def quarter_shift(yh, zh, edge):
    return 1 + yh + 2 * zh - edge + 8 * (1 - 2 * yh) + 32 * (1 - 2 * zh)


def pack_union(liquid, hydrate, speeds, count):
    x, z, y = coordinates(liquid.shape[0])
    core = (y >= 1) & (y <= 2) & (z >= 1) & (z <= 2)
    kept = []
    for value, edge in ((liquid, 0), (hydrate, 7)):
        for yh in range(2):
            for zh in range(2):
                value = jnp.where(core & (x == 1 + yh + 2 * zh), roll_lanes(speeds[0], quarter_shift(yh, zh, edge)), value)
        kept.append(value)
    lane = lax.broadcasted_iota(jnp.int32, liquid.shape, 1)
    kept[0] = jnp.where(lane == COUNT_LANE, count, kept[0])
    third = speeds[1]
    middle = (z >= 1) & (z <= 2)
    for zh in range(2):
        for far in range(2):
            third = jnp.where(middle & (y == 2 * zh + far),
                              roll_lanes(speeds[2], 32 * (1 - 2 * zh) + 8 * (2 * zh - 2 * far)), third)
    return kept[0], kept[1], third


def union_tables(first, second, third):
    rows = first.shape[0]
    coordinate = coordinates(rows)
    x, z, y = coordinate
    lane = lax.broadcasted_iota(jnp.int32, (rows, CELLS), 1)
    live = (lane.astype(F32) < first[:, COUNT_LANE:COUNT_LANE + 1]).astype(F32)
    tables = [jnp.zeros((rows, CELLS), F32) for _ in range(5)]
    for d in range(6):
        t, k = table_of[d], d // 2
        edge = axis_extent[k] - 1 if d % 2 == 0 else 0
        made = tables[t]
        for member, value in enumerate((first, second, None, live)):
            p = place_of(d, member)
            there = coordinate[k] == p
            if member != 2:
                made = jnp.where(there, roll_lanes(value, (p - edge) * axis_stride[k]), made)
            elif k == 0:
                held = second if edge else first
                for yh in range(2):
                    for zh in range(2):
                        made = jnp.where(there & ((y >> 1) == yh) & ((z >> 1) == zh),
                                         roll_lanes(held, p - edge - quarter_shift(yh, zh, edge)), made)
            elif k == 1:
                made = jnp.where(there, roll_lanes(third, (p - edge) * 32), made)
            else:
                far = 1 if edge else 0
                for zh in range(2):
                    made = jnp.where(there & ((z >> 1) == zh),
                                     roll_lanes(third, 8 * (p - 2 * zh - far) - 32 * (1 - 2 * zh)), made)
        tables[t] = made
    return tables


def kernel(na, nv, frac, mot, home, cnt, nb, phase, rates, fout, mout,
           cells, mv_send, mv_recv, mv_pay, vt_send, ax_send, ax_recv, vt_recv, win, acc, rowbuf, cols,
           mv_ss, mv_rs, ax_ss, ax_rs, vt_ss, vt_rs):
    slots = frac.shape[1]
    shift = slots.bit_length() - 1
    total = slots * na
    ax, vt = lax.axis_index("ax"), lax.axis_index("vt")

    def inside(a, v):
        return (a >= 0) & (a < na) & (v >= 0) & (v < nv)

    barrier = pltpu.get_barrier_semaphore()
    others = [(i, j) for i in (-1, 0, 1) for j in (-1, 0, 1) if (i, j) != (0, 0)]
    greeted = 0
    for i, j in others:
        there = inside(ax + i, vt + j)
        greeted = greeted + there.astype(jnp.int32)

        @pl.when(there)
        def _():
            pl.semaphore_signal(barrier, inc=1, device_id=(ax + i, vt + j), device_id_type=MESH)

    steps = (1, -1)

    def mover(s, peer):
        return pltpu.make_async_remote_copy(
            src_ref=mv_send.at[s], dst_ref=mv_recv.at[s], send_sem=mv_ss.at[s], recv_sem=mv_rs.at[s],
            device_id=peer, device_id_type=MESH)

    def axial(s, v, peer):
        return pltpu.make_async_remote_copy(
            src_ref=ax_send.at[s], dst_ref=ax_recv.at[s * 3 + v], send_sem=ax_ss.at[s * 3 + v],
            recv_sem=ax_rs.at[s * 3 + v], device_id=peer, device_id_type=MESH)

    piece = slots // PIECES

    def vertical(s, q, peer):
        return pltpu.make_async_remote_copy(
            src_ref=vt_send.at[q], dst_ref=vt_recv.at[s * PIECES + q], send_sem=vt_ss.at[s * PIECES + q],
            recv_sem=vt_rs.at[s * PIECES + q], device_id=peer, device_id_type=MESH)

    slot_row = lax.broadcasted_iota(jnp.int32, (1, slots), 1)
    target = home[...]
    target_ax = (target >> shift) & (na - 1)
    linked = nb[...]
    linked_ax = jnp.where(linked >= 0, (linked >> shift) & (na - 1), -5)
    masks = [(target_ax == ax + 1), (target_ax == ax - 1)]
    reach_up = jnp.max((linked_ax == ax + 1).astype(jnp.int32), axis=0, keepdims=True) > 0
    reach_down = jnp.max((linked_ax == ax - 1).astype(jnp.int32), axis=0, keepdims=True) > 0
    masks += [reach_up & (slot_row < slots - SPAN), reach_down & (slot_row >= SPAN)]
    masks = [m.astype(F32) for m in masks]
    mask8 = jnp.concatenate(masks + [jnp.zeros((4, slots), F32)], axis=0)
    before = lax.broadcasted_iota(jnp.int32, (slots, slots), 0) < lax.broadcasted_iota(jnp.int32, (slots, slots), 1)
    rank = jnp.dot(mask8.astype(BF16), before.astype(F32).astype(BF16), preferred_element_type=F32)
    rank = jnp.where(mask8 > 0.0, rank, -1.0)

    def one_hot(which, rows):
        m = (lax.broadcasted_iota(jnp.int32, (rows, slots), 0) & (MOVES - 1)).astype(F32)
        return (rank[which:which + 1] == m).astype(F32)

    def names(which, row):
        return lax.dot_general(
            jnp.broadcast_to(row, (8, slots)), one_hot(which, CELLS), (((1,), (1,)), ((), ())),
            precision=HIGH, preferred_element_type=F32)

    target_slot = (target & (slots - 1)).astype(F32) + 1.0
    global_row = (slot_row + (vt * total + ax * slots)).astype(F32) + 1.0
    pick = jnp.concatenate([one_hot(0, MOVES), one_hot(1, MOVES)], axis=0)
    for f in range(6):
        source = frac[f] if f < 2 else mot[f - 2]
        packed = jnp.dot(pick, source, precision=HIGH, preferred_element_type=F32)
        for s in range(2):
            mv_send[s, f * MOVES:(f + 1) * MOVES] = packed[s * MOVES:(s + 1) * MOVES]
    for s in range(2):
        mv_send[s, 6 * MOVES:] = names(s, target_slot)

    pl.semaphore_wait(barrier, greeted)
    for s in range(2):
        @pl.when(inside(ax + steps[s], vt))
        def _():
            mover(s, (ax + steps[s], vt)).start()

    rowbuf[...] = jnp.concatenate(
        [linked.astype(F32), cnt[...].astype(F32), jnp.zeros((1, slots), F32)], axis=0)
    cols[...] = rowbuf[...].T

    for s in range(2):
        ax_send[s, 3 * PACK:] = names(2 + s, global_row)

    for s in range(2):
        @pl.when(jnp.logical_not(inside(ax - steps[s], vt)))
        def _():
            mv_recv[s] = jnp.zeros((ROWS_MV, CELLS), F32)

        @pl.when(jnp.logical_not(inside(ax, vt - steps[s])))
        def _():
            for q in range(PIECES):
                vt_recv[s * PIECES + q] = jnp.zeros((3, piece, CELLS), F32)

        for v in range(3):
            @pl.when(jnp.logical_not(inside(ax - steps[s], vt - (v - 1))))
            def _():
                ax_recv[s * 3 + v] = jnp.zeros((ROWS_AX, CELLS), F32)

    mv_pay[...] = jnp.zeros_like(mv_pay)
    for s in range(2):
        @pl.when(inside(ax - steps[s], vt))
        def _():
            mover(s, (ax - steps[s], vt)).wait_recv()

    lane1 = lax.broadcasted_iota(jnp.int32, (1, CELLS), 1)
    arrivals = jnp.where(lane1 < MOVES, mv_recv[0, 6 * MOVES:6 * MOVES + 1],
                         jnp.where(lane1 < 2 * MOVES, mv_recv[1, 6 * MOVES:6 * MOVES + 1], 0.0)) - 1.0
    for f in range(6):
        for s in range(2):
            mv_pay[f, s * MOVES:(s + 1) * MOVES] = mv_recv[s, f * MOVES:(f + 1) * MOVES]

    chunk = 64

    def settle(q, c):
        start = pl.multiple_of(q * piece + c * chunk, chunk)
        part = pl.ds(pl.multiple_of(c * chunk, chunk), chunk)
        rows = pl.ds(start, chunk)
        at = (lax.broadcasted_iota(jnp.int32, (chunk, CELLS), 0) + start).astype(F32)
        select = (at == arrivals).astype(F32)
        hit = jnp.max(select, axis=1, keepdims=True) > 0.0
        lane = lax.broadcasted_iota(jnp.int32, (chunk, CELLS), 1)
        live = (lane.astype(F32) < cols[rows, 6:7]).astype(F32)
        now = []
        for f in range(6):
            old = frac[f, rows] if f < 2 else mot[f - 2, rows]
            came = jnp.dot(select, mv_pay[f], precision=HIGH, preferred_element_type=F32)
            value = jnp.where(hit, came, old)
            cells[f, rows] = value
            now.append(value)
            if f >= 2:
                mout[f - 2, rows] = value * live
        coordinate = coordinates(chunk)
        for t in range(5):
            made = jnp.zeros((chunk, CELLS), F32)
            for d in range(6):
                if table_of[d] != t:
                    continue
                k = d // 2
                edge = axis_extent[k] - 1 if d % 2 == 0 else 0
                for member, value in enumerate((now[0], now[1], now[2 + k], live)):
                    p = place_of(d, member)
                    made = jnp.where(coordinate[k] == p, roll_lanes(value, (p - edge) * axis_stride[k]), made)
            hi, lo = halves(made)
            win[t, rows, :CELLS] = hi
            win[t, rows, CELLS:] = lo
        union = pack_union(now[0], now[1], now[2:5], cols[rows, 6:7])
        for r in range(3):
            vt_send[q, r, part] = union[r]

    for q in range(PIECES):
        pl.loop(0, piece // chunk)(functools.partial(settle, q))
        for s in range(2):
            @pl.when(inside(ax, vt + steps[s]))
            def _():
                vertical(s, q, (ax, vt + steps[s])).start()

    pick = jnp.concatenate([one_hot(2, MOVES), one_hot(3, MOVES)], axis=0)
    for r in range(3):
        packed = jnp.zeros((2 * MOVES, CELLS), F32)
        for q in range(PIECES):
            packed = packed + jnp.dot(pick[:, q * piece:(q + 1) * piece], vt_send[q, r], precision=HIGH,
                                      preferred_element_type=F32)
        for s in range(2):
            ax_send[s, r * PACK:r * PACK + SPAN] = vt_send[PIECES - 1, r, piece - SPAN:] if s == 0 else vt_send[0, r, :SPAN]
            ax_send[s, r * PACK + SPAN:(r + 1) * PACK] = packed[s * MOVES:(s + 1) * MOVES]
    for s in range(2):
        for v in range(3):
            @pl.when(inside(ax + steps[s], vt + v - 1))
            def _():
                axial(s, v, (ax + steps[s], vt + v - 1)).start()

    def gather(t, keys, fresh):
        depth = keys.shape[1]
        for d in range(6):
            if table_of[d] != t:
                continue
            match = (cols[:, d:d + 1] == keys).astype(F32).astype(BF16)
            both = jnp.dot(match, win[t, :depth], preferred_element_type=F32)
            both = both[:, :CELLS] + both[:, CELLS:]
            if fresh:
                acc[d] = both
            else:
                acc[d] += both

    for t in range(5):
        gather(t, global_row - 1.0, True)

    for s in range(2):
        for v in range(3):
            @pl.when(inside(ax - steps[s], vt - (v - 1)))
            def _():
                axial(s, v, (ax - steps[s], vt - (v - 1))).wait_recv()
    layer_keys = jnp.full((1, slots), -2.0, F32)
    which = slot_row >> (SPAN.bit_length() - 1)
    within = slot_row & (SPAN - 1)
    for s in range(2):
        for v in range(3):
            w = s * 3 + v
            base = (vt - (v - 1)) * total + (ax - steps[s]) * slots + (slots - SPAN if s == 0 else 0)
            layer_keys = jnp.where(which == w, (within + base).astype(F32), layer_keys)
    other_keys = jnp.full((1, CELLS), -2.0, F32)
    for w in range(6):
        row = ax_recv[w, 3 * PACK:3 * PACK + 1]
        row = jnp.where(row > 0.0, row - 1.0, -2.0)
        other_keys = jnp.where((lane1 >> 4) == w, row, other_keys)
    ax_keys = jnp.concatenate([layer_keys[:, :6 * SPAN], other_keys], axis=1)

    @pl.loop(0, 6)
    def _(w):
        tables = union_tables(*[ax_recv[w, r * PACK:(r + 1) * PACK] for r in range(3)])
        layer = pl.ds(pl.multiple_of(w * SPAN, SPAN), SPAN)
        rest = pl.ds(pl.multiple_of(6 * SPAN + w * MOVES, MOVES), MOVES)
        for t in range(5):
            hi, lo = halves(tables[t])
            win[t, layer, :CELLS] = hi[:SPAN]
            win[t, layer, CELLS:] = lo[:SPAN]
            win[t, rest, :CELLS] = hi[SPAN:]
            win[t, rest, CELLS:] = lo[SPAN:]

    for t in range(5):
        win[t, 6 * PACK:] = jnp.zeros((slots - 6 * PACK, 2 * CELLS), BF16)
        gather(t, ax_keys, False)

    piece_row = lax.broadcasted_iota(jnp.int32, (1, piece), 1)
    unpack = 32
    for q in range(PIECES):
        keys = []
        for s in range(2):
            @pl.when(inside(ax, vt - steps[s]))
            def _():
                vertical(s, q, (ax, vt - steps[s])).wait_recv()

            @pl.loop(0, piece // unpack)
            def _(c):
                rows = pl.ds(pl.multiple_of(c * unpack, unpack), unpack)
                to = pl.ds(pl.multiple_of(s * piece + c * unpack, unpack), unpack)
                tables = union_tables(*[vt_recv[s * PIECES + q, r, rows] for r in range(3)])
                for t in range(5):
                    hi, lo = halves(tables[t])
                    win[t, to, :CELLS] = hi
                    win[t, to, CELLS:] = lo

            keys.append((piece_row + ((vt - steps[s]) * total + ax * slots + q * piece)).astype(F32))
        keys = jnp.concatenate(keys, axis=1)
        for t in range(5):
            gather(t, keys, False)

    small = 32

    @pl.loop(0, slots // small)
    def _(c):
        rows = pl.ds(pl.multiple_of(c * small, small), small)
        lane = lax.broadcasted_iota(jnp.int32, (small, CELLS), 1)
        live = (lane.astype(F32) < cols[rows, 6:7]).astype(F32)
        coordinate = coordinates(small)
        liquid, hydrate = cells[0, rows], cells[1, rows]
        flux_l = jnp.zeros((small, CELLS), F32)
        flux_h = jnp.zeros((small, CELLS), F32)
        for d in range(6):
            k = d // 2
            stride, extent = axis_stride[k], axis_extent[k]
            edge = 0 if d % 2 == 0 else extent - 1
            step = stride if d % 2 == 0 else -stride
            got = acc[d, rows]
            speed = cells[2 + k, rows]
            near = [
                jnp.where(coordinate[k] == edge, roll_lanes(got, (edge - place_of(d, m)) * stride), roll_lanes(value, step))
                for m, value in enumerate((liquid, hydrate, speed, live))
            ]
            outward = (1.0 if d % 2 else -1.0) * 0.5 * (speed + near[2])
            weight = live * near[3]
            out, into = weight * jnp.maximum(outward, 0.0), weight * jnp.minimum(outward, 0.0)
            flux_l = flux_l + (out * liquid + into * near[0])
            flux_h = flux_h + (out * hydrate + into * near[1])
        rate = jnp.zeros((small, CELLS), F32)
        kinds = phase[rows]
        for kind in range(rates.shape[0]):
            rate = jnp.where(kinds == kind, rates[kind], rate)
        growth = rate * cells[5, rows] * liquid * (1.0 - hydrate)
        fout[0, rows] = live * (liquid - time_step * flux_l - time_step * growth)
        fout[1, rows] = live * (hydrate - time_step * flux_h + time_step * growth)

    for s in range(2):
        @pl.when(inside(ax + steps[s], vt))
        def _():
            mover(s, (ax + steps[s], vt)).wait_send()

        for v in range(3):
            @pl.when(inside(ax + steps[s], vt + v - 1))
            def _():
                axial(s, v, (ax + steps[s], vt + v - 1)).wait_send()

        for q in range(PIECES):
            @pl.when(inside(ax, vt + steps[s]))
            def _():
                vertical(s, q, (ax, vt + steps[s])).wait_send()


def on_device(fractions, motion_fields, new_home, counts, neighbours, phase_ids, growth_rates):
    na, nv = lax.axis_size("ax"), lax.axis_size("vt")
    slots = fractions.shape[2]
    vmem = pl.BlockSpec(memory_space=pltpu.VMEM)
    fout, mout = pl.pallas_call(
        functools.partial(kernel, na, nv),
        out_shape=(jax.ShapeDtypeStruct((2, slots, CELLS), F32), jax.ShapeDtypeStruct((4, slots, CELLS), F32)),
        in_specs=[vmem] * 6 + [pl.BlockSpec(memory_space=pltpu.SMEM)],
        out_specs=(vmem, vmem),
        scratch_shapes=[
            pltpu.VMEM((6, slots, CELLS), F32),
            pltpu.VMEM((2, ROWS_MV, CELLS), F32),
            pltpu.VMEM((2, ROWS_MV, CELLS), F32),
            pltpu.VMEM((6, CELLS, CELLS), F32),
            pltpu.VMEM((PIECES, 3, slots // PIECES, CELLS), F32),
            pltpu.VMEM((2, ROWS_AX, CELLS), F32),
            pltpu.VMEM((6, ROWS_AX, CELLS), F32),
            pltpu.VMEM((2 * PIECES, 3, slots // PIECES, CELLS), F32),
            pltpu.VMEM((5, slots, 2 * CELLS), BF16),
            pltpu.VMEM((6, slots, CELLS), F32),
            pltpu.VMEM((8, slots), F32),
            pltpu.VMEM((slots, 8), F32),
            pltpu.SemaphoreType.DMA((2,)),
            pltpu.SemaphoreType.DMA((2,)),
            pltpu.SemaphoreType.DMA((6,)),
            pltpu.SemaphoreType.DMA((6,)),
            pltpu.SemaphoreType.DMA((2 * PIECES,)),
            pltpu.SemaphoreType.DMA((2 * PIECES,)),
        ],
        compiler_params=pltpu.CompilerParams(
            collective_id=0, has_side_effects=True, vmem_limit_bytes=40 * 1024 * 1024),
    )(fractions[:, 0], motion_fields[:, 0], new_home, counts, neighbours[:, 0], phase_ids[0], growth_rates)
    return fout[:, None], mout[:, None]


def solution(mesh):
    in_specs = (
        P(None, "vt", "ax", None),
        P(None, "vt", "ax", None),
        P("vt", "ax"),
        P("vt", "ax"),
        P(None, "vt", "ax"),
        P("vt", "ax", None),
        P(),
    )
    out_specs = (P(None, "vt", "ax", None), P(None, "vt", "ax", None))
    return jax.shard_map(
        on_device, mesh=mesh, in_specs=in_specs, out_specs=out_specs, check_vma=False
    )
```

```python
import functools

import jax
import jax.numpy as jnp
from jax import lax
from jax.experimental import pallas as pl
from jax.experimental.pallas import tpu as pltpu
from jax.sharding import PartitionSpec as P

MOVES = 16
SPAN = 64
CELLS = 128
MESH = pl.DeviceIdType.MESH
HIGH = lax.Precision.HIGHEST
F32 = jnp.float32
BF16 = jnp.bfloat16

axis_stride = (1, 32, 8)
axis_extent = (8, 4, 4)
time_step = 0.25
table_of = (0, 0, 1, 2, 3, 4)
PACK = SPAN + MOVES
ROWS_AX = 3 * PACK + 8
ROWS_MV = 6 * MOVES + 8
ROWS_FIX = 6 * MOVES + 24


def place_of(direction, member):
    return member + (4 if direction == 1 else 0)


def roll_lanes(x, shift):
    shift = shift % CELLS
    return x if shift == 0 else pltpu.roll(x, shift, 1)


def coordinates(rows):
    lane = lax.broadcasted_iota(jnp.int32, (rows, CELLS), 1)
    return (lane & 7, (lane >> 5) & 3, (lane >> 3) & 3)


def halves(x):
    hi = x.astype(BF16)
    return hi, (x - hi.astype(F32)).astype(BF16)


PIECES = 4
COUNT_LANE = 45


def quarter_shift(yh, zh, edge):
    return 1 + yh + 2 * zh - edge + 8 * (1 - 2 * yh) + 32 * (1 - 2 * zh)


def pack_union(liquid, hydrate, speeds, count):
    x, z, y = coordinates(liquid.shape[0])
    core = (y >= 1) & (y <= 2) & (z >= 1) & (z <= 2)
    kept = []
    for value, edge in ((liquid, 0), (hydrate, 7)):
        for yh in range(2):
            for zh in range(2):
                value = jnp.where(core & (x == 1 + yh + 2 * zh), roll_lanes(speeds[0], quarter_shift(yh, zh, edge)), value)
        kept.append(value)
    lane = lax.broadcasted_iota(jnp.int32, liquid.shape, 1)
    kept[0] = jnp.where(lane == COUNT_LANE, count, kept[0])
    third = speeds[1]
    middle = (z >= 1) & (z <= 2)
    for zh in range(2):
        for far in range(2):
            third = jnp.where(middle & (y == 2 * zh + far),
                              roll_lanes(speeds[2], 32 * (1 - 2 * zh) + 8 * (2 * zh - 2 * far)), third)
    return kept[0], kept[1], third


def union_tables(first, second, third):
    rows = first.shape[0]
    coordinate = coordinates(rows)
    x, z, y = coordinate
    lane = lax.broadcasted_iota(jnp.int32, (rows, CELLS), 1)
    live = (lane.astype(F32) < first[:, COUNT_LANE:COUNT_LANE + 1]).astype(F32)
    tables = [jnp.zeros((rows, CELLS), F32) for _ in range(5)]
    for d in range(6):
        t, k = table_of[d], d // 2
        edge = axis_extent[k] - 1 if d % 2 == 0 else 0
        made = tables[t]
        for member, value in enumerate((first, second, None, live)):
            p = place_of(d, member)
            there = coordinate[k] == p
            if member != 2:
                made = jnp.where(there, roll_lanes(value, (p - edge) * axis_stride[k]), made)
            elif k == 0:
                held = second if edge else first
                for yh in range(2):
                    for zh in range(2):
                        made = jnp.where(there & ((y >> 1) == yh) & ((z >> 1) == zh),
                                         roll_lanes(held, p - edge - quarter_shift(yh, zh, edge)), made)
            elif k == 1:
                made = jnp.where(there, roll_lanes(third, (p - edge) * 32), made)
            else:
                far = 1 if edge else 0
                for zh in range(2):
                    made = jnp.where(there & ((z >> 1) == zh),
                                     roll_lanes(third, 8 * (p - 2 * zh - far) - 32 * (1 - 2 * zh)), made)
        tables[t] = made
    return tables


def kernel(na, nv, frac, mot, home, cnt, nb, phase, rates, fout, mout,
           cells, mv_send, mv_recv, mv_pay, vt_send, settled, fix_send, fix_recv, ax_send, ax_recv, vt_recv, win, acc, rowbuf, cols,
           fix_ss, fix_rs, mv_ss, mv_rs, ax_ss, ax_rs, vt_ss, vt_rs):
    slots = frac.shape[1]
    shift = slots.bit_length() - 1
    total = slots * na
    ax, vt = lax.axis_index("ax"), lax.axis_index("vt")

    def inside(a, v):
        return (a >= 0) & (a < na) & (v >= 0) & (v < nv)

    barrier = pltpu.get_barrier_semaphore()
    others = [(i, j) for i in (-1, 0, 1) for j in (-1, 0, 1) if (i, j) != (0, 0)]
    greeted = 0
    for i, j in others:
        there = inside(ax + i, vt + j)
        greeted = greeted + there.astype(jnp.int32)

        @pl.when(there)
        def _():
            pl.semaphore_signal(barrier, inc=1, device_id=(ax + i, vt + j), device_id_type=MESH)

    steps = (1, -1)

    def mover(s, peer):
        return pltpu.make_async_remote_copy(
            src_ref=mv_send.at[s], dst_ref=mv_recv.at[s], send_sem=mv_ss.at[s], recv_sem=mv_rs.at[s],
            device_id=peer, device_id_type=MESH)

    def axial(s, v, peer):
        return pltpu.make_async_remote_copy(
            src_ref=ax_send.at[s], dst_ref=ax_recv.at[s * 3 + v], send_sem=ax_ss.at[s * 3 + v],
            recv_sem=ax_rs.at[s * 3 + v], device_id=peer, device_id_type=MESH)

    piece = slots // PIECES

    def vertical(s, q, peer):
        return pltpu.make_async_remote_copy(
            src_ref=vt_send.at[q], dst_ref=vt_recv.at[s * PIECES + q], send_sem=vt_ss.at[s * PIECES + q],
            recv_sem=vt_rs.at[s * PIECES + q], device_id=peer, device_id_type=MESH)

    def fixes(s, peer):
        return pltpu.make_async_remote_copy(
            src_ref=fix_send, dst_ref=fix_recv.at[s], send_sem=fix_ss.at[s], recv_sem=fix_rs.at[s],
            device_id=peer, device_id_type=MESH)

    slot_row = lax.broadcasted_iota(jnp.int32, (1, slots), 1)
    target = home[...]
    target_ax = (target >> shift) & (na - 1)
    linked = nb[...]
    linked_ax = jnp.where(linked >= 0, (linked >> shift) & (na - 1), -5)
    masks = [(target_ax == ax + 1), (target_ax == ax - 1)]
    reach_up = jnp.max((linked_ax == ax + 1).astype(jnp.int32), axis=0, keepdims=True) > 0
    reach_down = jnp.max((linked_ax == ax - 1).astype(jnp.int32), axis=0, keepdims=True) > 0
    masks += [reach_up & (slot_row < slots - SPAN), reach_down & (slot_row >= SPAN)]
    masks = [m.astype(F32) for m in masks]
    mask8 = jnp.concatenate(masks + [jnp.zeros((4, slots), F32)], axis=0)
    before = lax.broadcasted_iota(jnp.int32, (slots, slots), 0) < lax.broadcasted_iota(jnp.int32, (slots, slots), 1)
    rank = jnp.dot(mask8.astype(BF16), before.astype(F32).astype(BF16), preferred_element_type=F32)
    rank = jnp.where(mask8 > 0.0, rank, -1.0)

    def one_hot(which, rows):
        m = (lax.broadcasted_iota(jnp.int32, (rows, slots), 0) & (MOVES - 1)).astype(F32)
        return (rank[which:which + 1] == m).astype(F32)

    def names(which, row):
        return lax.dot_general(
            jnp.broadcast_to(row, (8, slots)), one_hot(which, CELLS), (((1,), (1,)), ((), ())),
            precision=HIGH, preferred_element_type=F32)

    target_slot = (target & (slots - 1)).astype(F32) + 1.0
    global_row = (slot_row + (vt * total + ax * slots)).astype(F32) + 1.0
    pick = jnp.concatenate([one_hot(0, MOVES), one_hot(1, MOVES)], axis=0)
    for f in range(6):
        source = frac[f] if f < 2 else mot[f - 2]
        packed = jnp.dot(pick, source, precision=HIGH, preferred_element_type=F32)
        for s in range(2):
            mv_send[s, f * MOVES:(f + 1) * MOVES] = packed[s * MOVES:(s + 1) * MOVES]
    for s in range(2):
        mv_send[s, 6 * MOVES:] = names(s, target_slot)

    pl.semaphore_wait(barrier, greeted)
    for s in range(2):
        @pl.when(inside(ax + steps[s], vt))
        def _():
            mover(s, (ax + steps[s], vt)).start()

    rowbuf[...] = jnp.concatenate(
        [linked.astype(F32), cnt[...].astype(F32), jnp.zeros((1, slots), F32)], axis=0)
    cols[...] = rowbuf[...].T

    early = 64
    for q in range(PIECES):
        @pl.loop(0, piece // early)
        def _(c):
            rows = pl.ds(pl.multiple_of(q * piece + c * early, early), early)
            part = pl.ds(pl.multiple_of(c * early, early), early)
            union = pack_union(frac[0, rows], frac[1, rows], [mot[k, rows] for k in range(3)], cols[rows, 6:7])
            for r in range(3):
                vt_send[q, r, part] = union[r]

        for s in range(2):
            @pl.when(inside(ax, vt + steps[s]))
            def _():
                vertical(s, q, (ax, vt + steps[s])).start()

    for s in range(2):
        ax_send[s, 3 * PACK:] = names(2 + s, global_row)

    for s in range(2):
        @pl.when(jnp.logical_not(inside(ax - steps[s], vt)))
        def _():
            mv_recv[s] = jnp.zeros((ROWS_MV, CELLS), F32)

        @pl.when(jnp.logical_not(inside(ax, vt - steps[s])))
        def _():
            for q in range(PIECES):
                vt_recv[s * PIECES + q] = jnp.zeros((3, piece, CELLS), F32)

        for v in range(3):
            @pl.when(jnp.logical_not(inside(ax - steps[s], vt - (v - 1))))
            def _():
                ax_recv[s * 3 + v] = jnp.zeros((ROWS_AX, CELLS), F32)

    mv_pay[...] = jnp.zeros_like(mv_pay)
    for s in range(2):
        @pl.when(inside(ax - steps[s], vt))
        def _():
            mover(s, (ax - steps[s], vt)).wait_recv()

    lane1 = lax.broadcasted_iota(jnp.int32, (1, CELLS), 1)
    arrivals = jnp.where(lane1 < MOVES, mv_recv[0, 6 * MOVES:6 * MOVES + 1],
                         jnp.where(lane1 < 2 * MOVES, mv_recv[1, 6 * MOVES:6 * MOVES + 1], 0.0)) - 1.0
    for f in range(6):
        for s in range(2):
            mv_pay[f, s * MOVES:(s + 1) * MOVES] = mv_recv[s, f * MOVES:(f + 1) * MOVES]

    chunk = 64

    def settle(q, c):
        start = pl.multiple_of(q * piece + c * chunk, chunk)
        part = pl.ds(pl.multiple_of(c * chunk, chunk), chunk)
        rows = pl.ds(start, chunk)
        at = (lax.broadcasted_iota(jnp.int32, (chunk, CELLS), 0) + start).astype(F32)
        select = (at == arrivals).astype(F32)
        hit = jnp.max(select, axis=1, keepdims=True) > 0.0
        lane = lax.broadcasted_iota(jnp.int32, (chunk, CELLS), 1)
        live = (lane.astype(F32) < cols[rows, 6:7]).astype(F32)
        now = []
        for f in range(6):
            old = frac[f, rows] if f < 2 else mot[f - 2, rows]
            came = jnp.dot(select, mv_pay[f], precision=HIGH, preferred_element_type=F32)
            value = jnp.where(hit, came, old)
            cells[f, rows] = value
            now.append(value)
            if f >= 2:
                mout[f - 2, rows] = value * live
        coordinate = coordinates(chunk)
        for t in range(5):
            made = jnp.zeros((chunk, CELLS), F32)
            for d in range(6):
                if table_of[d] != t:
                    continue
                k = d // 2
                edge = axis_extent[k] - 1 if d % 2 == 0 else 0
                for member, value in enumerate((now[0], now[1], now[2 + k], live)):
                    p = place_of(d, member)
                    made = jnp.where(coordinate[k] == p, roll_lanes(value, (p - edge) * axis_stride[k]), made)
            hi, lo = halves(made)
            win[t, rows, :CELLS] = hi
            win[t, rows, CELLS:] = lo
        union = pack_union(now[0], now[1], now[2:5], cols[rows, 6:7])
        for r in range(3):
            settled[q, r, part] = union[r]

    for q in range(PIECES):
        pl.loop(0, piece // chunk)(functools.partial(settle, q))

    pick = jnp.concatenate([one_hot(2, MOVES), one_hot(3, MOVES), one_hot(0, MOVES), one_hot(1, MOVES)], axis=0)
    for r in range(3):
        packed = jnp.zeros((4 * MOVES, CELLS), F32)
        for q in range(PIECES):
            packed = packed + jnp.dot(pick[:, q * piece:(q + 1) * piece], settled[q, r], precision=HIGH,
                                      preferred_element_type=F32)
        for s in range(2):
            ax_send[s, r * PACK:r * PACK + SPAN] = settled[PIECES - 1, r, piece - SPAN:] if s == 0 else settled[0, r, :SPAN]
            ax_send[s, r * PACK + SPAN:(r + 1) * PACK] = packed[s * MOVES:(s + 1) * MOVES]
        fix_send[r * 2 * MOVES:(r + 1) * 2 * MOVES] = packed[2 * MOVES:]
    for s in range(2):
        fix_send[6 * MOVES + 8 * s:6 * MOVES + 8 * s + 8] = names(s, global_row)
    replaced = masks[0] + masks[1]
    fix_send[6 * MOVES + 16:] = jnp.concatenate(
        [replaced[:, q * piece:(q + 1) * piece] for q in range(PIECES)] + [jnp.zeros((8 - PIECES, piece), F32)], axis=0)
    for s in range(2):
        @pl.when(inside(ax, vt + steps[s]))
        def _():
            fixes(s, (ax, vt + steps[s])).start()

        @pl.when(jnp.logical_not(inside(ax, vt - steps[s])))
        def _():
            fix_recv[s] = jnp.zeros((ROWS_FIX, CELLS), F32)
    for s in range(2):
        for v in range(3):
            @pl.when(inside(ax + steps[s], vt + v - 1))
            def _():
                axial(s, v, (ax + steps[s], vt + v - 1)).start()

    def gather(t, keys, fresh):
        depth = keys.shape[1]
        for d in range(6):
            if table_of[d] != t:
                continue
            match = (cols[:, d:d + 1] == keys).astype(F32).astype(BF16)
            both = jnp.dot(match, win[t, :depth], preferred_element_type=F32)
            both = both[:, :CELLS] + both[:, CELLS:]
            if fresh:
                acc[d] = both
            else:
                acc[d] += both

    for t in range(5):
        gather(t, global_row - 1.0, True)

    for s in range(2):
        for v in range(3):
            @pl.when(inside(ax - steps[s], vt - (v - 1)))
            def _():
                axial(s, v, (ax - steps[s], vt - (v - 1))).wait_recv()
    layer_keys = jnp.full((1, slots), -2.0, F32)
    which = slot_row >> (SPAN.bit_length() - 1)
    within = slot_row & (SPAN - 1)
    for s in range(2):
        for v in range(3):
            w = s * 3 + v
            base = (vt - (v - 1)) * total + (ax - steps[s]) * slots + (slots - SPAN if s == 0 else 0)
            layer_keys = jnp.where(which == w, (within + base).astype(F32), layer_keys)
    other_keys = jnp.full((1, CELLS), -2.0, F32)
    for w in range(6):
        row = ax_recv[w, 3 * PACK:3 * PACK + 1]
        row = jnp.where(row > 0.0, row - 1.0, -2.0)
        other_keys = jnp.where((lane1 >> 4) == w, row, other_keys)
    ax_keys = jnp.concatenate([layer_keys[:, :6 * SPAN], other_keys], axis=1)

    @pl.loop(0, 6)
    def _(w):
        tables = union_tables(*[ax_recv[w, r * PACK:(r + 1) * PACK] for r in range(3)])
        layer = pl.ds(pl.multiple_of(w * SPAN, SPAN), SPAN)
        rest = pl.ds(pl.multiple_of(6 * SPAN + w * MOVES, MOVES), MOVES)
        for t in range(5):
            hi, lo = halves(tables[t])
            win[t, layer, :CELLS] = hi[:SPAN]
            win[t, layer, CELLS:] = lo[:SPAN]
            win[t, rest, :CELLS] = hi[SPAN:]
            win[t, rest, CELLS:] = lo[SPAN:]

    for t in range(5):
        win[t, 6 * PACK:] = jnp.zeros((slots - 6 * PACK, 2 * CELLS), BF16)
        gather(t, ax_keys, False)

    fix_keys = jnp.full((1, CELLS), -2.0, F32)
    for s in range(2):
        @pl.when(inside(ax, vt - steps[s]))
        def _():
            fixes(s, (ax, vt - steps[s])).wait_recv()

        tables = union_tables(*[fix_recv[s, r * 2 * MOVES:(r + 1) * 2 * MOVES] for r in range(3)])
        for t in range(5):
            hi, lo = halves(tables[t])
            win[t, s * 2 * MOVES:(s + 1) * 2 * MOVES, :CELLS] = hi
            win[t, s * 2 * MOVES:(s + 1) * 2 * MOVES, CELLS:] = lo
        for way in range(2):
            row = fix_recv[s, 6 * MOVES + 8 * way:6 * MOVES + 8 * way + 1]
            row = jnp.where(row > 0.0, row - 1.0, -2.0)
            fix_keys = jnp.where((lane1 >> 4) == 2 * s + way, row, fix_keys)
    for t in range(5):
        win[t, 4 * MOVES:CELLS] = jnp.zeros((CELLS - 4 * MOVES, 2 * CELLS), BF16)
        gather(t, fix_keys, False)

    piece_row = lax.broadcasted_iota(jnp.int32, (1, piece), 1)
    unpack = 32
    for q in range(PIECES):
        keys = []
        for s in range(2):
            @pl.when(inside(ax, vt - steps[s]))
            def _():
                vertical(s, q, (ax, vt - steps[s])).wait_recv()

            @pl.loop(0, piece // unpack)
            def _(c):
                rows = pl.ds(pl.multiple_of(c * unpack, unpack), unpack)
                to = pl.ds(pl.multiple_of(s * piece + c * unpack, unpack), unpack)
                tables = union_tables(*[vt_recv[s * PIECES + q, r, rows] for r in range(3)])
                for t in range(5):
                    hi, lo = halves(tables[t])
                    win[t, to, :CELLS] = hi
                    win[t, to, CELLS:] = lo

            named = (piece_row + ((vt - steps[s]) * total + ax * slots + q * piece)).astype(F32)
            keys.append(jnp.where(fix_recv[s, 6 * MOVES + 16 + q:6 * MOVES + 17 + q] > 0.0, -2.0, named))
        keys = jnp.concatenate(keys, axis=1)
        for t in range(5):
            gather(t, keys, False)

    small = 32

    @pl.loop(0, slots // small)
    def _(c):
        rows = pl.ds(pl.multiple_of(c * small, small), small)
        lane = lax.broadcasted_iota(jnp.int32, (small, CELLS), 1)
        live = (lane.astype(F32) < cols[rows, 6:7]).astype(F32)
        coordinate = coordinates(small)
        liquid, hydrate = cells[0, rows], cells[1, rows]
        flux_l = jnp.zeros((small, CELLS), F32)
        flux_h = jnp.zeros((small, CELLS), F32)
        for d in range(6):
            k = d // 2
            stride, extent = axis_stride[k], axis_extent[k]
            edge = 0 if d % 2 == 0 else extent - 1
            step = stride if d % 2 == 0 else -stride
            got = acc[d, rows]
            speed = cells[2 + k, rows]
            near = [
                jnp.where(coordinate[k] == edge, roll_lanes(got, (edge - place_of(d, m)) * stride), roll_lanes(value, step))
                for m, value in enumerate((liquid, hydrate, speed, live))
            ]
            outward = (1.0 if d % 2 else -1.0) * 0.5 * (speed + near[2])
            weight = live * near[3]
            out, into = weight * jnp.maximum(outward, 0.0), weight * jnp.minimum(outward, 0.0)
            flux_l = flux_l + (out * liquid + into * near[0])
            flux_h = flux_h + (out * hydrate + into * near[1])
        rate = jnp.zeros((small, CELLS), F32)
        kinds = phase[rows]
        for kind in range(rates.shape[0]):
            rate = jnp.where(kinds == kind, rates[kind], rate)
        growth = rate * cells[5, rows] * liquid * (1.0 - hydrate)
        fout[0, rows] = live * (liquid - time_step * flux_l - time_step * growth)
        fout[1, rows] = live * (hydrate - time_step * flux_h + time_step * growth)

    for s in range(2):
        @pl.when(inside(ax + steps[s], vt))
        def _():
            mover(s, (ax + steps[s], vt)).wait_send()

        for v in range(3):
            @pl.when(inside(ax + steps[s], vt + v - 1))
            def _():
                axial(s, v, (ax + steps[s], vt + v - 1)).wait_send()

        @pl.when(inside(ax, vt + steps[s]))
        def _():
            fixes(s, (ax, vt + steps[s])).wait_send()

        for q in range(PIECES):
            @pl.when(inside(ax, vt + steps[s]))
            def _():
                vertical(s, q, (ax, vt + steps[s])).wait_send()


def on_device(fractions, motion_fields, new_home, counts, neighbours, phase_ids, growth_rates):
    na, nv = lax.axis_size("ax"), lax.axis_size("vt")
    slots = fractions.shape[2]
    vmem = pl.BlockSpec(memory_space=pltpu.VMEM)
    fout, mout = pl.pallas_call(
        functools.partial(kernel, na, nv),
        out_shape=(jax.ShapeDtypeStruct((2, slots, CELLS), F32), jax.ShapeDtypeStruct((4, slots, CELLS), F32)),
        in_specs=[vmem] * 6 + [pl.BlockSpec(memory_space=pltpu.SMEM)],
        out_specs=(vmem, vmem),
        scratch_shapes=[
            pltpu.VMEM((6, slots, CELLS), F32),
            pltpu.VMEM((2, ROWS_MV, CELLS), F32),
            pltpu.VMEM((2, ROWS_MV, CELLS), F32),
            pltpu.VMEM((6, CELLS, CELLS), F32),
            pltpu.VMEM((PIECES, 3, slots // PIECES, CELLS), F32),
            pltpu.VMEM((PIECES, 3, slots // PIECES, CELLS), F32),
            pltpu.VMEM((ROWS_FIX, CELLS), F32),
            pltpu.VMEM((2, ROWS_FIX, CELLS), F32),
            pltpu.VMEM((2, ROWS_AX, CELLS), F32),
            pltpu.VMEM((6, ROWS_AX, CELLS), F32),
            pltpu.VMEM((2 * PIECES, 3, slots // PIECES, CELLS), F32),
            pltpu.VMEM((5, slots, 2 * CELLS), BF16),
            pltpu.VMEM((6, slots, CELLS), F32),
            pltpu.VMEM((8, slots), F32),
            pltpu.VMEM((slots, 8), F32),
            pltpu.SemaphoreType.DMA((2,)),
            pltpu.SemaphoreType.DMA((2,)),
            pltpu.SemaphoreType.DMA((2,)),
            pltpu.SemaphoreType.DMA((2,)),
            pltpu.SemaphoreType.DMA((6,)),
            pltpu.SemaphoreType.DMA((6,)),
            pltpu.SemaphoreType.DMA((2 * PIECES,)),
            pltpu.SemaphoreType.DMA((2 * PIECES,)),
        ],
        compiler_params=pltpu.CompilerParams(
            collective_id=0, has_side_effects=True, vmem_limit_bytes=40 * 1024 * 1024),
    )(fractions[:, 0], motion_fields[:, 0], new_home, counts, neighbours[:, 0], phase_ids[0], growth_rates)
    return fout[:, None], mout[:, None]


def solution(mesh):
    in_specs = (
        P(None, "vt", "ax", None),
        P(None, "vt", "ax", None),
        P("vt", "ax"),
        P("vt", "ax"),
        P(None, "vt", "ax"),
        P("vt", "ax", None),
        P(),
    )
    out_specs = (P(None, "vt", "ax", None), P(None, "vt", "ax", None))
    return jax.shard_map(
        on_device, mesh=mesh, in_specs=in_specs, out_specs=out_specs, check_vma=False
    )
```

```python
import functools

import jax
import jax.numpy as jnp
from jax import lax
from jax.experimental import pallas as pl
from jax.experimental.pallas import tpu as pltpu
from jax.sharding import PartitionSpec as P

MOVES = 16
SPAN = 64
CELLS = 128
MESH = pl.DeviceIdType.MESH
HIGH = lax.Precision.HIGHEST
F32 = jnp.float32
BF16 = jnp.bfloat16

axis_stride = (1, 32, 8)
axis_extent = (8, 4, 4)
time_step = 0.25
table_of = (0, 0, 1, 2, 3, 4)
PACK = SPAN + MOVES
ROWS_AX = 3 * PACK + 8
ROWS_MV = 6 * MOVES + 8
ROWS_FIX = 6 * MOVES + 24


def place_of(direction, member):
    return member + (4 if direction == 1 else 0)


def roll_lanes(x, shift):
    shift = shift % CELLS
    return x if shift == 0 else pltpu.roll(x, shift, 1)


def coordinates(rows):
    lane = lax.broadcasted_iota(jnp.int32, (rows, CELLS), 1)
    return (lane & 7, (lane >> 5) & 3, (lane >> 3) & 3)


def halves(x):
    hi = x.astype(BF16)
    return hi, (x - hi.astype(F32)).astype(BF16)


PIECES = 4
COUNT_LANE = 45


def quarter_shift(yh, zh, edge):
    return 1 + yh + 2 * zh - edge + 8 * (1 - 2 * yh) + 32 * (1 - 2 * zh)


def pack_union(liquid, hydrate, speeds, count):
    x, z, y = coordinates(liquid.shape[0])
    core = (y >= 1) & (y <= 2) & (z >= 1) & (z <= 2)
    kept = []
    for value, edge in ((liquid, 0), (hydrate, 7)):
        for yh in range(2):
            for zh in range(2):
                value = jnp.where(core & (x == 1 + yh + 2 * zh), roll_lanes(speeds[0], quarter_shift(yh, zh, edge)), value)
        kept.append(value)
    lane = lax.broadcasted_iota(jnp.int32, liquid.shape, 1)
    kept[0] = jnp.where(lane == COUNT_LANE, count, kept[0])
    third = speeds[1]
    middle = (z >= 1) & (z <= 2)
    for zh in range(2):
        for far in range(2):
            third = jnp.where(middle & (y == 2 * zh + far),
                              roll_lanes(speeds[2], 32 * (1 - 2 * zh) + 8 * (2 * zh - 2 * far)), third)
    return kept[0], kept[1], third


def union_tables(first, second, third):
    rows = first.shape[0]
    coordinate = coordinates(rows)
    x, z, y = coordinate
    lane = lax.broadcasted_iota(jnp.int32, (rows, CELLS), 1)
    live = (lane.astype(F32) < first[:, COUNT_LANE:COUNT_LANE + 1]).astype(F32)
    tables = [jnp.zeros((rows, CELLS), F32) for _ in range(5)]
    for d in range(6):
        t, k = table_of[d], d // 2
        edge = axis_extent[k] - 1 if d % 2 == 0 else 0
        made = tables[t]
        for member, value in enumerate((first, second, None, live)):
            p = place_of(d, member)
            there = coordinate[k] == p
            if member != 2:
                made = jnp.where(there, roll_lanes(value, (p - edge) * axis_stride[k]), made)
            elif k == 0:
                held = second if edge else first
                for yh in range(2):
                    for zh in range(2):
                        made = jnp.where(there & ((y >> 1) == yh) & ((z >> 1) == zh),
                                         roll_lanes(held, p - edge - quarter_shift(yh, zh, edge)), made)
            elif k == 1:
                made = jnp.where(there, roll_lanes(third, (p - edge) * 32), made)
            else:
                far = 1 if edge else 0
                for zh in range(2):
                    made = jnp.where(there & ((z >> 1) == zh),
                                     roll_lanes(third, 8 * (p - 2 * zh - far) - 32 * (1 - 2 * zh)), made)
        tables[t] = made
    return tables


def kernel(na, nv, frac, mot, home, cnt, nb, phase, rates, fout, mout,
           cells, mv_send, mv_recv, mv_pay, vt_send, settled, fix_send, fix_recv, ax_send, ax_recv, vt_recv, win, acc, rowbuf, cols,
           fix_ss, fix_rs, mv_ss, mv_rs, ax_ss, ax_rs, vt_ss, vt_rs):
    slots = frac.shape[1]
    shift = slots.bit_length() - 1
    total = slots * na
    ax, vt = lax.axis_index("ax"), lax.axis_index("vt")

    def inside(a, v):
        return (a >= 0) & (a < na) & (v >= 0) & (v < nv)

    barrier = pltpu.get_barrier_semaphore()
    others = [(i, j) for i in (-1, 0, 1) for j in (-1, 0, 1) if (i, j) != (0, 0)]
    greeted = 0
    for i, j in others:
        there = inside(ax + i, vt + j)
        greeted = greeted + there.astype(jnp.int32)

        @pl.when(there)
        def _():
            pl.semaphore_signal(barrier, inc=1, device_id=(ax + i, vt + j), device_id_type=MESH)

    steps = (1, -1)

    def mover(s, peer):
        return pltpu.make_async_remote_copy(
            src_ref=mv_send.at[s], dst_ref=mv_recv.at[s], send_sem=mv_ss.at[s], recv_sem=mv_rs.at[s],
            device_id=peer, device_id_type=MESH)

    def axial(s, v, peer):
        return pltpu.make_async_remote_copy(
            src_ref=ax_send.at[s], dst_ref=ax_recv.at[s * 3 + v], send_sem=ax_ss.at[s * 3 + v],
            recv_sem=ax_rs.at[s * 3 + v], device_id=peer, device_id_type=MESH)

    piece = slots // PIECES

    def vertical(s, q, peer):
        return pltpu.make_async_remote_copy(
            src_ref=vt_send.at[q], dst_ref=vt_recv.at[s * PIECES + q], send_sem=vt_ss.at[s * PIECES + q],
            recv_sem=vt_rs.at[s * PIECES + q], device_id=peer, device_id_type=MESH)

    def fixes(s, peer):
        return pltpu.make_async_remote_copy(
            src_ref=fix_send, dst_ref=fix_recv.at[s], send_sem=fix_ss.at[s], recv_sem=fix_rs.at[s],
            device_id=peer, device_id_type=MESH)

    slot_row = lax.broadcasted_iota(jnp.int32, (1, slots), 1)
    target = home[...]
    target_ax = (target >> shift) & (na - 1)
    linked = nb[...]
    linked_ax = jnp.where(linked >= 0, (linked >> shift) & (na - 1), -5)
    masks = [(target_ax == ax + 1), (target_ax == ax - 1)]
    reach_up = jnp.max((linked_ax == ax + 1).astype(jnp.int32), axis=0, keepdims=True) > 0
    reach_down = jnp.max((linked_ax == ax - 1).astype(jnp.int32), axis=0, keepdims=True) > 0
    masks += [reach_up & (slot_row < slots - SPAN), reach_down & (slot_row >= SPAN)]
    masks = [m.astype(F32) for m in masks]
    mask8 = jnp.concatenate(masks + [jnp.zeros((4, slots), F32)], axis=0)
    before = lax.broadcasted_iota(jnp.int32, (slots, slots), 0) < lax.broadcasted_iota(jnp.int32, (slots, slots), 1)
    rank = jnp.dot(mask8.astype(BF16), before.astype(F32).astype(BF16), preferred_element_type=F32)
    rank = jnp.where(mask8 > 0.0, rank, -1.0)

    def one_hot(which, rows):
        m = (lax.broadcasted_iota(jnp.int32, (rows, slots), 0) & (MOVES - 1)).astype(F32)
        return (rank[which:which + 1] == m).astype(F32)

    def names(which, row):
        return lax.dot_general(
            jnp.broadcast_to(row, (8, slots)), one_hot(which, CELLS), (((1,), (1,)), ((), ())),
            precision=HIGH, preferred_element_type=F32)

    target_slot = (target & (slots - 1)).astype(F32) + 1.0
    global_row = (slot_row + (vt * total + ax * slots)).astype(F32) + 1.0
    pick = jnp.concatenate([one_hot(0, MOVES), one_hot(1, MOVES)], axis=0)
    for f in range(6):
        source = frac[f] if f < 2 else mot[f - 2]
        packed = jnp.dot(pick, source, precision=HIGH, preferred_element_type=F32)
        for s in range(2):
            mv_send[s, f * MOVES:(f + 1) * MOVES] = packed[s * MOVES:(s + 1) * MOVES]
    for s in range(2):
        mv_send[s, 6 * MOVES:] = names(s, target_slot)

    pl.semaphore_wait(barrier, greeted)
    for s in range(2):
        @pl.when(inside(ax + steps[s], vt))
        def _():
            mover(s, (ax + steps[s], vt)).start()

    rowbuf[...] = jnp.concatenate(
        [linked.astype(F32), cnt[...].astype(F32), jnp.zeros((1, slots), F32)], axis=0)
    cols[...] = rowbuf[...].T

    early = 64
    for q in range(PIECES):
        @pl.loop(0, piece // early)
        def _(c):
            rows = pl.ds(pl.multiple_of(q * piece + c * early, early), early)
            part = pl.ds(pl.multiple_of(c * early, early), early)
            union = pack_union(frac[0, rows], frac[1, rows], [mot[k, rows] for k in range(3)], cols[rows, 6:7])
            for r in range(3):
                vt_send[q, r, part] = union[r]

        for s in range(2):
            @pl.when(inside(ax, vt + steps[s]))
            def _():
                vertical(s, q, (ax, vt + steps[s])).start()

    for s in range(2):
        ax_send[s, 3 * PACK:] = names(2 + s, global_row)

    for s in range(2):
        @pl.when(jnp.logical_not(inside(ax - steps[s], vt)))
        def _():
            mv_recv[s] = jnp.zeros((ROWS_MV, CELLS), F32)

        @pl.when(jnp.logical_not(inside(ax, vt - steps[s])))
        def _():
            for q in range(PIECES):
                vt_recv[s * PIECES + q] = jnp.zeros((3, piece, CELLS), F32)

        for v in range(3):
            @pl.when(jnp.logical_not(inside(ax - steps[s], vt - (v - 1))))
            def _():
                ax_recv[s * 3 + v] = jnp.zeros((ROWS_AX, CELLS), F32)

    mv_pay[...] = jnp.zeros_like(mv_pay)
    for s in range(2):
        @pl.when(inside(ax - steps[s], vt))
        def _():
            mover(s, (ax - steps[s], vt)).wait_recv()

    lane1 = lax.broadcasted_iota(jnp.int32, (1, CELLS), 1)
    arrivals = jnp.where(lane1 < MOVES, mv_recv[0, 6 * MOVES:6 * MOVES + 1],
                         jnp.where(lane1 < 2 * MOVES, mv_recv[1, 6 * MOVES:6 * MOVES + 1], 0.0)) - 1.0
    for f in range(6):
        for s in range(2):
            mv_pay[f, s * MOVES:(s + 1) * MOVES] = mv_recv[s, f * MOVES:(f + 1) * MOVES]

    chunk = 64

    def settle(q, c):
        start = pl.multiple_of(q * piece + c * chunk, chunk)
        part = pl.ds(pl.multiple_of(c * chunk, chunk), chunk)
        rows = pl.ds(start, chunk)
        at = (lax.broadcasted_iota(jnp.int32, (chunk, CELLS), 0) + start).astype(F32)
        select = (at == arrivals).astype(F32)
        hit = jnp.max(select, axis=1, keepdims=True) > 0.0
        lane = lax.broadcasted_iota(jnp.int32, (chunk, CELLS), 1)
        live = (lane.astype(F32) < cols[rows, 6:7]).astype(F32)
        now = []
        for f in range(6):
            old = frac[f, rows] if f < 2 else mot[f - 2, rows]
            came = jnp.dot(select, mv_pay[f], precision=HIGH, preferred_element_type=F32)
            value = jnp.where(hit, came, old)
            cells[f, rows] = value
            now.append(value)
            if f >= 2:
                mout[f - 2, rows] = value * live
        coordinate = coordinates(chunk)
        for t in range(5):
            made = jnp.zeros((chunk, CELLS), F32)
            for d in range(6):
                if table_of[d] != t:
                    continue
                k = d // 2
                edge = axis_extent[k] - 1 if d % 2 == 0 else 0
                for member, value in enumerate((now[0], now[1], now[2 + k], live)):
                    p = place_of(d, member)
                    made = jnp.where(coordinate[k] == p, roll_lanes(value, (p - edge) * axis_stride[k]), made)
            hi, lo = halves(made)
            win[t, rows, :CELLS] = hi
            win[t, rows, CELLS:] = lo
        union = pack_union(now[0], now[1], now[2:5], cols[rows, 6:7])
        for r in range(3):
            settled[q, r, part] = union[r]

    for q in range(PIECES):
        pl.loop(0, piece // chunk)(functools.partial(settle, q))

    pick = jnp.concatenate([one_hot(2, MOVES), one_hot(3, MOVES), one_hot(0, MOVES), one_hot(1, MOVES)], axis=0)
    for r in range(3):
        packed = jnp.zeros((4 * MOVES, CELLS), F32)
        for q in range(PIECES):
            packed = packed + jnp.dot(pick[:, q * piece:(q + 1) * piece], settled[q, r], precision=HIGH,
                                      preferred_element_type=F32)
        for s in range(2):
            ax_send[s, r * PACK:r * PACK + SPAN] = settled[PIECES - 1, r, piece - SPAN:] if s == 0 else settled[0, r, :SPAN]
            ax_send[s, r * PACK + SPAN:(r + 1) * PACK] = packed[s * MOVES:(s + 1) * MOVES]
        fix_send[r * 2 * MOVES:(r + 1) * 2 * MOVES] = packed[2 * MOVES:]
    for s in range(2):
        fix_send[6 * MOVES + 8 * s:6 * MOVES + 8 * s + 8] = names(s, global_row)
    replaced = masks[0] + masks[1]
    fix_send[6 * MOVES + 16:] = jnp.concatenate(
        [replaced[:, q * piece:(q + 1) * piece] for q in range(PIECES)] + [jnp.zeros((8 - PIECES, piece), F32)], axis=0)
    for s in range(2):
        @pl.when(inside(ax, vt + steps[s]))
        def _():
            fixes(s, (ax, vt + steps[s])).start()

        @pl.when(jnp.logical_not(inside(ax, vt - steps[s])))
        def _():
            fix_recv[s] = jnp.zeros((ROWS_FIX, CELLS), F32)
    for s in range(2):
        for v in range(3):
            @pl.when(inside(ax + steps[s], vt + v - 1))
            def _():
                axial(s, v, (ax + steps[s], vt + v - 1)).start()

    def gather(t, keys, fresh):
        depth = keys.shape[1]
        for d in range(6):
            if table_of[d] != t:
                continue
            match = (cols[:, d:d + 1] == keys).astype(F32).astype(BF16)
            both = jnp.dot(match, win[t, :depth], preferred_element_type=F32)
            both = both[:, :CELLS] + both[:, CELLS:]
            if fresh:
                acc[d] = both
            else:
                acc[d] += both

    for t in range(5):
        gather(t, global_row - 1.0, True)

    fix_keys = jnp.full((1, CELLS), -2.0, F32)
    for s in range(2):
        @pl.when(inside(ax, vt - steps[s]))
        def _():
            fixes(s, (ax, vt - steps[s])).wait_recv()

        tables = union_tables(*[fix_recv[s, r * 2 * MOVES:(r + 1) * 2 * MOVES] for r in range(3)])
        for t in range(5):
            hi, lo = halves(tables[t])
            win[t, s * 2 * MOVES:(s + 1) * 2 * MOVES, :CELLS] = hi
            win[t, s * 2 * MOVES:(s + 1) * 2 * MOVES, CELLS:] = lo
        for way in range(2):
            row = fix_recv[s, 6 * MOVES + 8 * way:6 * MOVES + 8 * way + 1]
            row = jnp.where(row > 0.0, row - 1.0, -2.0)
            fix_keys = jnp.where((lane1 >> 4) == 2 * s + way, row, fix_keys)
    for t in range(5):
        win[t, 4 * MOVES:CELLS] = jnp.zeros((CELLS - 4 * MOVES, 2 * CELLS), BF16)
        gather(t, fix_keys, False)

    piece_row = lax.broadcasted_iota(jnp.int32, (1, piece), 1)
    unpack = 32
    for q in range(PIECES):
        keys = []
        for s in range(2):
            @pl.when(inside(ax, vt - steps[s]))
            def _():
                vertical(s, q, (ax, vt - steps[s])).wait_recv()

            @pl.loop(0, piece // unpack)
            def _(c):
                rows = pl.ds(pl.multiple_of(c * unpack, unpack), unpack)
                to = pl.ds(pl.multiple_of(s * piece + c * unpack, unpack), unpack)
                tables = union_tables(*[vt_recv[s * PIECES + q, r, rows] for r in range(3)])
                for t in range(5):
                    hi, lo = halves(tables[t])
                    win[t, to, :CELLS] = hi
                    win[t, to, CELLS:] = lo

            named = (piece_row + ((vt - steps[s]) * total + ax * slots + q * piece)).astype(F32)
            keys.append(jnp.where(fix_recv[s, 6 * MOVES + 16 + q:6 * MOVES + 17 + q] > 0.0, -2.0, named))
        keys = jnp.concatenate(keys, axis=1)
        for t in range(5):
            gather(t, keys, False)

    for s in range(2):
        for v in range(3):
            @pl.when(inside(ax - steps[s], vt - (v - 1)))
            def _():
                axial(s, v, (ax - steps[s], vt - (v - 1))).wait_recv()
    layer_keys = jnp.full((1, slots), -2.0, F32)
    which = slot_row >> (SPAN.bit_length() - 1)
    within = slot_row & (SPAN - 1)
    for s in range(2):
        for v in range(3):
            w = s * 3 + v
            base = (vt - (v - 1)) * total + (ax - steps[s]) * slots + (slots - SPAN if s == 0 else 0)
            layer_keys = jnp.where(which == w, (within + base).astype(F32), layer_keys)
    other_keys = jnp.full((1, CELLS), -2.0, F32)
    for w in range(6):
        row = ax_recv[w, 3 * PACK:3 * PACK + 1]
        row = jnp.where(row > 0.0, row - 1.0, -2.0)
        other_keys = jnp.where((lane1 >> 4) == w, row, other_keys)
    ax_keys = jnp.concatenate([layer_keys[:, :6 * SPAN], other_keys], axis=1)

    @pl.loop(0, 6)
    def _(w):
        tables = union_tables(*[ax_recv[w, r * PACK:(r + 1) * PACK] for r in range(3)])
        layer = pl.ds(pl.multiple_of(w * SPAN, SPAN), SPAN)
        rest = pl.ds(pl.multiple_of(6 * SPAN + w * MOVES, MOVES), MOVES)
        for t in range(5):
            hi, lo = halves(tables[t])
            win[t, layer, :CELLS] = hi[:SPAN]
            win[t, layer, CELLS:] = lo[:SPAN]
            win[t, rest, :CELLS] = hi[SPAN:]
            win[t, rest, CELLS:] = lo[SPAN:]

    for t in range(5):
        win[t, 6 * PACK:] = jnp.zeros((slots - 6 * PACK, 2 * CELLS), BF16)
        gather(t, ax_keys, False)

    small = 32

    @pl.loop(0, slots // small)
    def _(c):
        rows = pl.ds(pl.multiple_of(c * small, small), small)
        lane = lax.broadcasted_iota(jnp.int32, (small, CELLS), 1)
        live = (lane.astype(F32) < cols[rows, 6:7]).astype(F32)
        coordinate = coordinates(small)
        liquid, hydrate = cells[0, rows], cells[1, rows]
        flux_l = jnp.zeros((small, CELLS), F32)
        flux_h = jnp.zeros((small, CELLS), F32)
        for d in range(6):
            k = d // 2
            stride, extent = axis_stride[k], axis_extent[k]
            edge = 0 if d % 2 == 0 else extent - 1
            step = stride if d % 2 == 0 else -stride
            got = acc[d, rows]
            speed = cells[2 + k, rows]
            near = [
                jnp.where(coordinate[k] == edge, roll_lanes(got, (edge - place_of(d, m)) * stride), roll_lanes(value, step))
                for m, value in enumerate((liquid, hydrate, speed, live))
            ]
            outward = (1.0 if d % 2 else -1.0) * 0.5 * (speed + near[2])
            weight = live * near[3]
            out, into = weight * jnp.maximum(outward, 0.0), weight * jnp.minimum(outward, 0.0)
            flux_l = flux_l + (out * liquid + into * near[0])
            flux_h = flux_h + (out * hydrate + into * near[1])
        rate = jnp.zeros((small, CELLS), F32)
        kinds = phase[rows]
        for kind in range(rates.shape[0]):
            rate = jnp.where(kinds == kind, rates[kind], rate)
        growth = rate * cells[5, rows] * liquid * (1.0 - hydrate)
        fout[0, rows] = live * (liquid - time_step * flux_l - time_step * growth)
        fout[1, rows] = live * (hydrate - time_step * flux_h + time_step * growth)

    for s in range(2):
        @pl.when(inside(ax + steps[s], vt))
        def _():
            mover(s, (ax + steps[s], vt)).wait_send()

        for v in range(3):
            @pl.when(inside(ax + steps[s], vt + v - 1))
            def _():
                axial(s, v, (ax + steps[s], vt + v - 1)).wait_send()

        @pl.when(inside(ax, vt + steps[s]))
        def _():
            fixes(s, (ax, vt + steps[s])).wait_send()

        for q in range(PIECES):
            @pl.when(inside(ax, vt + steps[s]))
            def _():
                vertical(s, q, (ax, vt + steps[s])).wait_send()


def on_device(fractions, motion_fields, new_home, counts, neighbours, phase_ids, growth_rates):
    na, nv = lax.axis_size("ax"), lax.axis_size("vt")
    slots = fractions.shape[2]
    vmem = pl.BlockSpec(memory_space=pltpu.VMEM)
    fout, mout = pl.pallas_call(
        functools.partial(kernel, na, nv),
        out_shape=(jax.ShapeDtypeStruct((2, slots, CELLS), F32), jax.ShapeDtypeStruct((4, slots, CELLS), F32)),
        in_specs=[vmem] * 6 + [pl.BlockSpec(memory_space=pltpu.SMEM)],
        out_specs=(vmem, vmem),
        scratch_shapes=[
            pltpu.VMEM((6, slots, CELLS), F32),
            pltpu.VMEM((2, ROWS_MV, CELLS), F32),
            pltpu.VMEM((2, ROWS_MV, CELLS), F32),
            pltpu.VMEM((6, CELLS, CELLS), F32),
            pltpu.VMEM((PIECES, 3, slots // PIECES, CELLS), F32),
            pltpu.VMEM((PIECES, 3, slots // PIECES, CELLS), F32),
            pltpu.VMEM((ROWS_FIX, CELLS), F32),
            pltpu.VMEM((2, ROWS_FIX, CELLS), F32),
            pltpu.VMEM((2, ROWS_AX, CELLS), F32),
            pltpu.VMEM((6, ROWS_AX, CELLS), F32),
            pltpu.VMEM((2 * PIECES, 3, slots // PIECES, CELLS), F32),
            pltpu.VMEM((5, slots, 2 * CELLS), BF16),
            pltpu.VMEM((6, slots, CELLS), F32),
            pltpu.VMEM((8, slots), F32),
            pltpu.VMEM((slots, 8), F32),
            pltpu.SemaphoreType.DMA((2,)),
            pltpu.SemaphoreType.DMA((2,)),
            pltpu.SemaphoreType.DMA((2,)),
            pltpu.SemaphoreType.DMA((2,)),
            pltpu.SemaphoreType.DMA((6,)),
            pltpu.SemaphoreType.DMA((6,)),
            pltpu.SemaphoreType.DMA((2 * PIECES,)),
            pltpu.SemaphoreType.DMA((2 * PIECES,)),
        ],
        compiler_params=pltpu.CompilerParams(
            collective_id=0, has_side_effects=True, vmem_limit_bytes=40 * 1024 * 1024),
    )(fractions[:, 0], motion_fields[:, 0], new_home, counts, neighbours[:, 0], phase_ids[0], growth_rates)
    return fout[:, None], mout[:, None]


def solution(mesh):
    in_specs = (
        P(None, "vt", "ax", None),
        P(None, "vt", "ax", None),
        P("vt", "ax"),
        P("vt", "ax"),
        P(None, "vt", "ax"),
        P("vt", "ax", None),
        P(),
    )
    out_specs = (P(None, "vt", "ax", None), P(None, "vt", "ax", None))
    return jax.shard_map(
        on_device, mesh=mesh, in_specs=in_specs, out_specs=out_specs, check_vma=False
    )
```
